128 devices in a mesh: row: 8 (over z, core), col: 8 (over x_lo, y), rep: 2 (over x_hi).
Axes of the slice: x: 4 (x_hi: 2, x_lo: 2; x = x_hi * 2 + x_lo), y: 4, z: 4, core: 2. Of those that a mesh axis runs over, the one named last changes fastest.
Arguments:
- pair: bfloat16 [1024, 512, 128], P(('rep', 'row'), 'col'), parts along dimension 0, may hold values from -6 to 6
- length: int32 [2], P('rep'), parts along dimension 0, may hold values from 128 to 512
- ln_in_gain: float32 [128], replicated, may hold values from 0.1 to 1.9
- ln_in_bias: float32 [128], replicated, may hold values from -1.2 to 1.2
- w_left: bfloat16 [128, 256], replicated, may hold values from -0.5 to 0.5
- w_right: bfloat16 [128, 256], replicated, may hold values from -0.5 to 0.5
- w_gate: bfloat16 [128, 128], replicated, may hold values from -0.5 to 0.5
- product_norm_gain: float32 [128], replicated, may hold values from 0.1 to 1.9
- product_norm_bias: float32 [128], replicated, may hold values from -1.2 to 1.2
- w_out: bfloat16 [128, 128], replicated, may hold values from -0.5 to 0.5
- cotangent: bfloat16 [1024, 512, 128], P(('rep', 'row'), 'col'), parts along dimension 0, may hold values from -6 to 6
Outputs:
- updated: bfloat16 [1024, 512, 128], P(('rep', 'row'), 'col'), parts along dimension 0
- d_pair: bfloat16 [1024, 512, 128], P(('rep', 'row'), 'col'), parts along dimension 0
- grad_left: float32 [256, 256], P('rep'), parts along dimension 0
- grad_right: float32 [256, 256], P('rep'), parts along dimension 0
- grad_gate: float32 [256, 128], P('rep'), parts along dimension 0
- grad_out: float32 [256, 128], P('rep'), parts along dimension 0
The draws below stay inside these ranges and needn't reach their ends.
There are 2 independent parts, one for each index of `rep`. The reference program is written for one: setup_inputs(seed, part) draws one part's arguments, and reference() takes and returns one part's arrays. A program takes and returns all parts, laid end to end along the dimension named above; an argument that names none is the same for every part. Nothing has to cross between parts.
Inputs may be any that keep to these rules, and one draw needn't show every extreme that they name: Token i is valid when i < length.
All inputs are finite; a program needn't handle non-finite values.
Results may differ from the reference program's by a relative error of at most 0.02.
Values may be sent and summed in bfloat16 or wider, within the bound.
No kernel may reach another device: no remote copies, remote signals or barrier semaphores. Data moves between devices by JAX's collectives and lax.ppermute only.
A program may use at most 128 MiB of HBM per device.

```python
import jax
import jax.numpy as jnp
from jax import lax

C = 128
HID = 128
N = 512
N_ROW = 8
N_COL = 8


def level_of(key, extent, split, low, top_value):
    factor_of = 1.0
    for dim, parts in split:
        steps = jax.random.uniform(jax.random.fold_in(jax.random.fold_in(key, 6), dim), (parts,), jnp.float32, low / len(split), top_value / len(split))
        factor_of = factor_of * jnp.repeat(jnp.exp(steps), extent[dim] // parts).reshape((-1,) + (1,) * (len(extent) - 1 - dim))
    return factor_of


def noise(key, extent, spread, reach, shards=(), kind=jnp.bfloat16):
    result = jax.random.normal(key, extent, jnp.float32) * spread
    if len(shards) > 0:
        result = level_of(key, extent, shards, -0.22, 0.18) * result
    return jnp.clip(result, min=-reach, max=reach).astype(kind)


def setup_inputs(seed: int = 0, part: int = 0) -> dict:
    arg_keys = jax.random.split(jax.random.key(seed), 12)
    part_splits = jax.random.split(jax.random.fold_in(arg_keys[11], part), 12)
    return {
        "pair": noise(part_splits[0], (N, N, C), 1.0, 6.0, ((0, 8), (1, 8))),
        "length": jax.random.randint(part_splits[1], (1,), N // 4, N + 1).astype(jnp.int32),
        "ln_in_gain": jnp.clip(1.0 + 0.18 * jax.random.normal(arg_keys[2], (C,), jnp.float32), 0.1, 1.9),
        "ln_in_bias": noise(arg_keys[3], (C,), 0.3, 1.2, (), jnp.float32),
        "w_left": noise(arg_keys[4], (C, 2 * HID), C ** -0.5, 0.5),
        "w_right": noise(arg_keys[5], (C, 2 * HID), C ** -0.5, 0.5),
        "w_gate": noise(arg_keys[6], (C, C), C ** -0.5, 0.5),
        "product_norm_gain": jnp.clip(1.0 + 0.18 * jax.random.normal(arg_keys[7], (HID,), jnp.float32), 0.1, 1.9),
        "product_norm_bias": noise(arg_keys[8], (HID,), 0.3, 1.2, (), jnp.float32),
        "w_out": noise(arg_keys[9], (HID, C), HID ** -0.5, 0.5),
        "cotangent": noise(part_splits[10], (N, N, C), 1.0, 6.0, ((0, 8), (1, 8))),
    }


def apply_layer_norm(values):
    centered = values - lax.optimization_barrier(jnp.mean(values, axis=-1, keepdims=True))
    inverse = lax.rsqrt(lax.optimization_barrier(jnp.mean(centered * centered, axis=-1, keepdims=True)) + 1e-05)
    return (centered * inverse, inverse)

def layer_norm_backward(grad_hat, normed, inverse):
    return inverse * (grad_hat - lax.optimization_barrier(jnp.mean(grad_hat, axis=-1, keepdims=True)) - normed * lax.optimization_barrier(jnp.mean(grad_hat * normed, axis=-1, keepdims=True)))

def rounded(values):
    return lax.optimization_barrier(values.astype(jnp.bfloat16)).astype(jnp.float32)

def reference(pair, length, ln_in_gain, ln_in_bias, w_left, w_right, w_gate, product_norm_gain, product_norm_bias, w_out, cotangent):
    total = pair.shape[0]
    chans = pair.shape[2]
    hidden = w_out.shape[0]
    tile = total // N_COL
    valid = jnp.arange(total) < length[0]
    mask = (valid[:, None] & valid[None, :]).astype(jnp.float32)[..., None]
    zhat, inv_in = apply_layer_norm(pair.astype(jnp.float32))
    normed = (zhat * ln_in_gain + ln_in_bias).astype(jnp.bfloat16)
    flat = normed.reshape(-1, chans)
    left = jnp.dot(flat, w_left, preferred_element_type=jnp.float32).reshape(total, total, 2 * hidden)
    right = jnp.dot(flat, w_right, preferred_element_type=jnp.float32).reshape(total, total, 2 * hidden)
    sig_left = jax.nn.sigmoid(left[..., hidden:])
    sig_right = jax.nn.sigmoid(right[..., hidden:])
    a_val = (mask * sig_left * left[..., :hidden]).astype(jnp.bfloat16)
    b_val = (mask * sig_right * right[..., :hidden]).astype(jnp.bfloat16)
    gate = jax.nn.sigmoid(jnp.dot(flat, w_gate, preferred_element_type=jnp.float32).reshape(total, total, chans))
    a_wide = a_val.astype(jnp.float32)
    b_wide = b_val.astype(jnp.float32)
    triangle_product = jnp.zeros((total, total, hidden), jnp.float32)
    for block in range(N_COL):
        part_a = a_wide[:, block * tile:(block + 1) * tile]
        part_b = b_wide[:, block * tile:(block + 1) * tile]
        triangle_product = triangle_product + rounded(jnp.einsum('ikc,jkc->ijc', part_a, part_b))
    standardized_input, inverse_output_spread = apply_layer_norm(triangle_product)
    output_result = (standardized_input * product_norm_gain + product_norm_bias).astype(jnp.bfloat16)
    y_flat = output_result.reshape(-1, hidden)
    proj = jnp.dot(y_flat, w_out, preferred_element_type=jnp.float32).reshape(total, total, chans)
    updated = (gate * proj).astype(jnp.bfloat16)
    upstream = cotangent.astype(jnp.float32)
    d_proj = (upstream * gate).astype(jnp.bfloat16)
    d_gpre = (upstream * proj * gate * (1.0 - gate)).astype(jnp.bfloat16)
    d_proj_flat = d_proj.reshape(-1, chans)
    output_gradient = jnp.dot(d_proj_flat, w_out.T, preferred_element_type=jnp.float32).reshape(total, total, hidden)
    product_gradient = layer_norm_backward(output_gradient * product_norm_gain, standardized_input, inverse_output_spread).astype(jnp.bfloat16)
    d_prod_wide = product_gradient.astype(jnp.float32)
    d_a = jnp.einsum('ijc,jkc->ikc', d_prod_wide, b_wide)
    d_b = jnp.zeros((total, total, hidden), jnp.float32)
    for block in range(N_ROW):
        part_d = d_prod_wide[block * tile:(block + 1) * tile]
        part_a = a_wide[block * tile:(block + 1) * tile]
        d_b = d_b + rounded(jnp.einsum('ijc,ikc->jkc', part_d, part_a))
    d_left = jnp.concatenate([d_a * mask * sig_left, d_a * mask * left[..., :hidden] * sig_left * (1.0 - sig_left)], axis=-1).astype(jnp.bfloat16)
    d_right = jnp.concatenate([d_b * mask * sig_right, d_b * mask * right[..., :hidden] * sig_right * (1.0 - sig_right)], axis=-1).astype(jnp.bfloat16)
    d_left_flat = d_left.reshape(-1, 2 * hidden)
    d_right_flat = d_right.reshape(-1, 2 * hidden)
    d_gpre_flat = d_gpre.reshape(-1, chans)
    d_zn = (jnp.dot(d_left_flat, w_left.T, preferred_element_type=jnp.float32) + jnp.dot(d_right_flat, w_right.T, preferred_element_type=jnp.float32) + jnp.dot(d_gpre_flat, w_gate.T, preferred_element_type=jnp.float32)).reshape(total, total, chans)
    d_pair = layer_norm_backward(d_zn * ln_in_gain, zhat, inv_in).astype(jnp.bfloat16)
    scale = 1.0 / total
    grad_left = jnp.dot(flat.T, d_left_flat, preferred_element_type=jnp.float32) * scale
    grad_right = jnp.dot(flat.T, d_right_flat, preferred_element_type=jnp.float32) * scale
    grad_gate = jnp.dot(flat.T, d_gpre_flat, preferred_element_type=jnp.float32) * scale
    grad_out = jnp.dot(y_flat.T, d_proj_flat, preferred_element_type=jnp.float32) * scale
    return (updated, d_pair, grad_left, grad_right, grad_gate, grad_out)
```

```python
import jax
import jax.numpy as jnp
from jax import lax
from jax.sharding import PartitionSpec as P


AXES = ("row", "col")


def to_channels(tiles):
    count, tile_i, tile_j, chans = tiles.shape
    rows, cols = lax.axis_size("row"), lax.axis_size("col")
    parts = rows * cols
    send = tiles.reshape(count, tile_i, tile_j, parts, chans // parts)
    send = jnp.transpose(send, (3, 0, 4, 1, 2))
    got = lax.all_to_all(send, AXES, 0, 0, tiled=True)
    got = got.reshape(rows, cols, count, chans // parts, tile_i, tile_j)
    got = jnp.transpose(got, (2, 3, 0, 4, 1, 5))
    return got.reshape(count, chans // parts, rows * tile_i, cols * tile_j)


def to_cells(maps):
    count, owned, total_i, total_j = maps.shape
    rows, cols = lax.axis_size("row"), lax.axis_size("col")
    send = maps.reshape(count, owned, rows, total_i // rows, cols, total_j // cols)
    send = jnp.transpose(send, (2, 4, 0, 1, 3, 5))
    send = send.reshape(rows * cols, count, owned, total_i // rows, total_j // cols)
    got = lax.all_to_all(send, AXES, 0, 0, tiled=True)
    got = jnp.transpose(got, (1, 3, 4, 0, 2))
    return got.reshape(count, total_i // rows, total_j // cols, rows * cols * owned)


def apply_layer_norm(values):
    centered = values - jnp.mean(values, axis=-1, keepdims=True)
    inverse = lax.rsqrt(jnp.mean(centered * centered, axis=-1, keepdims=True) + 1e-05)
    return (centered * inverse, inverse)


def layer_norm_backward(grad_hat, normed, inverse):
    return inverse * (
        grad_hat
        - jnp.mean(grad_hat, axis=-1, keepdims=True)
        - normed * jnp.mean(grad_hat * normed, axis=-1, keepdims=True)
    )


def gated_grad(grad_val, mask, projected, sigma, hidden):
    value_part = grad_val * mask * sigma
    gate_part = grad_val * mask * projected[..., :hidden] * sigma * (1.0 - sigma)
    return jnp.concatenate([value_part, gate_part], axis=-1).astype(jnp.bfloat16)


def body(
    pair,
    length,
    ln_in_gain,
    ln_in_bias,
    w_left,
    w_right,
    w_gate,
    product_norm_gain,
    product_norm_bias,
    w_out,
    cotangent,
):
    tile_i, tile_j, chans = pair.shape
    hidden = w_out.shape[0]
    total = tile_j * lax.axis_size("col")
    row_first = lax.axis_index("row") * tile_i
    col_first = lax.axis_index("col") * tile_j
    row_valid = row_first + jnp.arange(tile_i) < length[0]
    col_valid = col_first + jnp.arange(tile_j) < length[0]
    mask = (row_valid[:, None] & col_valid[None, :]).astype(jnp.float32)[..., None]
    zhat, inv_in = apply_layer_norm(pair.astype(jnp.float32))
    normed = (zhat * ln_in_gain + ln_in_bias).astype(jnp.bfloat16)
    flat = normed.reshape(-1, chans)
    left = jnp.dot(flat, w_left, preferred_element_type=jnp.float32).reshape(
        tile_i, tile_j, 2 * hidden
    )
    right = jnp.dot(flat, w_right, preferred_element_type=jnp.float32).reshape(
        tile_i, tile_j, 2 * hidden
    )
    sig_left = jax.nn.sigmoid(left[..., hidden:])
    sig_right = jax.nn.sigmoid(right[..., hidden:])
    a_val = (mask * sig_left * left[..., :hidden]).astype(jnp.bfloat16)
    b_val = (mask * sig_right * right[..., :hidden]).astype(jnp.bfloat16)
    gate = jax.nn.sigmoid(
        jnp.dot(flat, w_gate, preferred_element_type=jnp.float32).reshape(tile_i, tile_j, chans)
    )
    full_a, full_b = to_channels(jnp.stack([a_val, b_val]))
    product = jnp.einsum("hik,hjk->hij", full_a, full_b, preferred_element_type=jnp.float32)
    triangle_product = to_cells(product.astype(jnp.bfloat16)[None])[0].astype(jnp.float32)
    standardized_input, inverse_output_spread = apply_layer_norm(triangle_product)
    output_result = (standardized_input * product_norm_gain + product_norm_bias).astype(
        jnp.bfloat16
    )
    y_flat = output_result.reshape(-1, hidden)
    proj = jnp.dot(y_flat, w_out, preferred_element_type=jnp.float32).reshape(tile_i, tile_j, chans)
    updated = (gate * proj).astype(jnp.bfloat16)
    upstream = cotangent.astype(jnp.float32)
    d_proj = (upstream * gate).astype(jnp.bfloat16)
    d_gpre = (upstream * proj * gate * (1.0 - gate)).astype(jnp.bfloat16)
    d_proj_flat = d_proj.reshape(-1, chans)
    output_gradient = jnp.dot(d_proj_flat, w_out.T, preferred_element_type=jnp.float32).reshape(
        tile_i, tile_j, hidden
    )
    product_gradient = layer_norm_backward(
        output_gradient * product_norm_gain, standardized_input, inverse_output_spread
    ).astype(jnp.bfloat16)
    full_d = to_channels(product_gradient[None])[0]
    full_da = jnp.einsum("hij,hjk->hik", full_d, full_b, preferred_element_type=jnp.float32)
    full_db = jnp.einsum("hij,hik->hjk", full_d, full_a, preferred_element_type=jnp.float32)
    d_a, d_b = to_cells(jnp.stack([full_da, full_db]).astype(jnp.bfloat16)).astype(jnp.float32)
    d_left = gated_grad(d_a, mask, left, sig_left, hidden)
    d_right = gated_grad(d_b, mask, right, sig_right, hidden)
    d_left_flat = d_left.reshape(-1, 2 * hidden)
    d_right_flat = d_right.reshape(-1, 2 * hidden)
    d_gpre_flat = d_gpre.reshape(-1, chans)
    d_zn = (
        jnp.dot(d_left_flat, w_left.T, preferred_element_type=jnp.float32)
        + jnp.dot(d_right_flat, w_right.T, preferred_element_type=jnp.float32)
        + jnp.dot(d_gpre_flat, w_gate.T, preferred_element_type=jnp.float32)
    ).reshape(tile_i, tile_j, chans)
    d_pair = layer_norm_backward(d_zn * ln_in_gain, zhat, inv_in).astype(jnp.bfloat16)
    term_left = jnp.dot(flat.T, d_left_flat, preferred_element_type=jnp.float32)
    term_right = jnp.dot(flat.T, d_right_flat, preferred_element_type=jnp.float32)
    term_gate = jnp.dot(flat.T, d_gpre_flat, preferred_element_type=jnp.float32)
    term_out = jnp.dot(y_flat.T, d_proj_flat, preferred_element_type=jnp.float32)
    terms = jnp.concatenate([term_left, term_right, term_gate, term_out], axis=1)
    shares = lax.all_to_all(terms.reshape(64, -1, 128), AXES, 0, 0, tiled=True)
    share = jnp.sum(shares, axis=0) * (1.0 / total)
    whole = lax.all_to_all(jnp.broadcast_to(share[None], shares.shape), AXES, 0, 0, tiled=True)
    whole = whole.reshape(chans, 6 * hidden)
    return (
        updated,
        d_pair,
        whole[:, : 2 * hidden],
        whole[:, 2 * hidden : 4 * hidden],
        whole[:, 4 * hidden : 5 * hidden],
        whole[:, 5 * hidden :],
    )


def solution(mesh):
    in_specs = (
        P(("rep", "row"), "col", None),
        P("rep"),
        P(),
        P(),
        P(),
        P(),
        P(),
        P(),
        P(),
        P(),
        P(("rep", "row"), "col", None),
    )
    out_specs = (
        P(("rep", "row"), "col", None),
        P(("rep", "row"), "col", None),
        P("rep", None),
        P("rep", None),
        P("rep", None),
        P("rep", None),
    )
    return jax.shard_map(body, mesh=mesh, in_specs=in_specs, out_specs=out_specs, check_vma=False)
```

```python
import functools

import jax
import jax.numpy as jnp
from jax import lax
from jax.experimental import pallas as pl
from jax.experimental.pallas import tpu as pltpu
from jax.sharding import PartitionSpec as P

AXES = ("row", "col")
BF = jnp.bfloat16
F32 = jnp.float32
STEP = 16
EPS = 1e-05


def dot(lhs, rhs, left_dim, right_dim):
    return lax.dot_general(
        lhs, rhs, (((left_dim,), (right_dim,)), ((), ())), preferred_element_type=F32
    )


def column(ref):
    return jnp.transpose(jnp.broadcast_to(ref[...], (128, 128)))[:, :1]


def normalize(values):
    centered = values - jnp.mean(values, axis=0, keepdims=True)
    inverse = lax.rsqrt(jnp.mean(centered * centered, axis=0, keepdims=True) + EPS)
    return centered * inverse, inverse


def normalize_backward(grad_hat, normed, inverse):
    return inverse * (
        grad_hat
        - jnp.mean(grad_hat, axis=0, keepdims=True)
        - normed * jnp.mean(grad_hat * normed, axis=0, keepdims=True)
    )


def load_transposed(ref):
    rows, cols, chans = ref.shape
    return jnp.transpose(ref[...].reshape(rows * cols, chans)).astype(F32)


def store_transposed(ref, values):
    rows, cols, chans = ref.shape
    ref[...] = jnp.transpose(values.astype(BF)).reshape(rows, cols, chans)


def low_half(shape):
    return lax.broadcasted_iota(jnp.int32, shape, len(shape) - 1) < 64


def pack(values, scr):
    low = low_half((64, 128))
    for t in range(STEP // 2):
        first = values[:64, t * 128 : (t + 1) * 128]
        second = values[64:, t * 128 : (t + 1) * 128]
        scr[pl.ds(2 * t, 64, stride=STEP), :] = jnp.where(low, first, pltpu.roll(second, 64, 1))
        scr[pl.ds(2 * t + 1, 64, stride=STEP), :] = jnp.where(
            low, pltpu.roll(first, 64, 1), second
        )
    return scr[...].reshape(64, STEP, 128).astype(BF)


def unpack(payload, scr):
    low = low_half((64, 128))
    scr[...] = payload.astype(F32).reshape(64 * STEP, 128)
    tiles = []
    for t in range(STEP // 2):
        even = scr[pl.ds(2 * t, 64, stride=STEP), :]
        odd = scr[pl.ds(2 * t + 1, 64, stride=STEP), :]
        first = jnp.where(low, even, pltpu.roll(odd, 64, 1))
        second = jnp.where(low, pltpu.roll(even, 64, 1), odd)
        tiles.append(jnp.concatenate([first, second], axis=0))
    return jnp.concatenate(tiles, axis=1)


def cell_mask(length_ref):
    cells = lax.broadcasted_iota(jnp.int32, (1, STEP * 64), 1)
    row = lax.axis_index("row") * 64 + pl.program_id(0) * STEP + cells // 64
    col = lax.axis_index("col") * 64 + cells % 64
    length = length_ref[0]
    return ((row < length) & (col < length)).astype(F32)


def operands_kernel(pair, length, gain, bias, w_left, w_right, send, zn_out, scr):
    zhat, _ = normalize(load_transposed(pair))
    zn = (zhat * column(gain) + column(bias)).astype(BF)
    zn_out[...] = zn
    mask = cell_mask(length)
    left = dot(w_left[...], zn, 0, 0)
    send[:, 0] = pack(mask * jax.nn.sigmoid(left[128:]) * left[:128], scr)
    right = dot(w_right[...], zn, 0, 0)
    send[:, 1] = pack(mask * jax.nn.sigmoid(right[128:]) * right[:128], scr)


def factors_kernel(zn, length, w_left, w_right, w_gate, cot, sl, gl, sr, gr, gate, cot_out):
    mask = cell_mask(length)
    gate[...] = jax.nn.sigmoid(dot(w_gate[...], zn[...], 0, 0))
    cot_out[...] = load_transposed(cot)
    for weights, slope, bend in ((w_left, sl, gl), (w_right, sr, gr)):
        value = dot(weights[...], zn[...], 0, 0)
        sigma = jax.nn.sigmoid(value[128:])
        slope[...] = mask * sigma
        bend[...] = mask * value[:128] * sigma * (1.0 - sigma)


def gather_map(got, which, scr):
    for r in range(8):
        for c in range(8):
            scr[r * 64 : (r + 1) * 64, c * 128 : (c + 1) * 128] = got[r * 8 + c, which]


def double_rows(got, which, scr):
    low = low_half((64, 128))
    zero = jnp.zeros((64, 128), BF)
    for r in range(8):
        for c in range(8):
            tile = got[r * 8 + c, which]
            lanes = slice(c * 128, (c + 1) * 128)
            scr[r * 128 : r * 128 + 64, lanes] = jnp.where(low, tile, zero)
            scr[r * 128 + 64 : (r + 1) * 128, lanes] = jnp.where(low, zero, tile)


def product_kernel(got, send, a_scr, b_scr):
    gather_map(got, 0, a_scr)
    double_rows(got, 1, b_scr)
    for n in range(4):
        out = dot(a_scr[...], b_scr[n * 256 : (n + 1) * 256, :], 1, 1).astype(BF)
        for r in range(8):
            for c in range(2):
                send[r * 8 + 2 * n + c] = out[r * 64 : (r + 1) * 64, c * 128 : (c + 1) * 128]


def middle_kernel(
    got, gate_ref, cot, zn, gain_ref, bias_ref, w_out,
    updated, send, dg_out, grad_out, grad_gate, scr,
):
    hat, inverse = normalize(unpack(got[...], scr))
    gain = column(gain_ref)
    y = (hat * gain + column(bias_ref)).astype(BF)
    proj = dot(w_out[...], y, 0, 0)
    gate = gate_ref[...]
    upstream = cot[...]
    d_proj = (upstream * gate).astype(BF)
    d_y = dot(w_out[...], d_proj, 1, 0)
    send[...] = pack(normalize_backward(d_y * gain, hat, inverse), scr)
    store_transposed(updated, gate * proj)
    d_gpre = (upstream * proj * gate * (1.0 - gate)).astype(BF)
    dg_out[...] = d_gpre

    @pl.when(pl.program_id(0) == 0)
    def _():
        grad_out[...] = jnp.zeros((128, 128), F32)
        grad_gate[...] = jnp.zeros((128, 128), F32)

    grad_out[...] += dot(y, d_proj, 1, 1)
    grad_gate[...] += dot(zn[...], d_gpre, 1, 1)


def product_grads_kernel(got, operands, send, a_scr, b_scr, d_scr):
    gather_map(operands, 0, a_scr)
    double_rows(operands, 1, b_scr)
    for r in range(8):
        for c in range(8):
            d_scr[r * 64 : (r + 1) * 64, c * 128 : (c + 1) * 128] = got[r * 8 + c]
    for n in range(4):
        out = dot(d_scr[...], b_scr[:, n * 256 : (n + 1) * 256], 1, 0).astype(BF)
        for r in range(8):
            for c in range(2):
                send[r * 8 + 2 * n + c, 0] = out[r * 64 : (r + 1) * 64, c * 128 : (c + 1) * 128]
    low = low_half((64, 128))
    for m in range(2):
        out = dot(d_scr[:, m * 512 : (m + 1) * 512], a_scr[...], 0, 0)
        for r in range(4):
            for c in range(8):
                lanes = slice(c * 128, (c + 1) * 128)
                send[(m * 4 + r) * 8 + c, 1] = jnp.where(
                    low, out[r * 128 : r * 128 + 64, lanes], out[r * 128 + 64 : (r + 1) * 128, lanes]
                ).astype(BF)


def weights_kernel(got, zn, sl, gl, sr, gr, grad_gate, grad_out, dl_out, dr_out, send, scr, acc):
    step = pl.program_id(0)
    z = zn[...]

    @pl.when(step == 0)
    def _():
        acc[...] = jnp.zeros((128, 512), F32)

    for which, slope, bend, out in ((0, sl, gl, dl_out), (1, sr, gr, dr_out)):
        grad = unpack(got[:, which], scr)
        value = jnp.concatenate([grad * slope[...], grad * bend[...]], axis=0).astype(BF)
        out[...] = value
        acc[:, which * 256 : (which + 1) * 256] += dot(z, value, 1, 1)

    @pl.when(step == pl.num_programs(0) - 1)
    def _():
        for t in range(6):
            if t < 4:
                tile = acc[:, t * 128 : (t + 1) * 128]
            else:
                tile = (grad_gate if t == 4 else grad_out)[...]
            for half in range(2):
                send[pl.ds(2 * t + half, 64, stride=16), :] = tile[half * 64 : (half + 1) * 64]
        for t in range(12, 16):
            send[pl.ds(t, 64, stride=16), :] = jnp.zeros((64, 128), F32)


def pair_kernel(pair, gain, dl, dr, dg, w_left, w_right, w_gate, out):
    zhat, inverse = normalize(load_transposed(pair))
    d_zn = (
        dot(w_left[...], dl[...], 1, 0)
        + dot(w_right[...], dr[...], 1, 0)
        + dot(w_gate[...], dg[...], 1, 0)
    )
    store_transposed(out, normalize_backward(d_zn * column(gain), zhat, inverse))


def sum_kernel(scale, got, send):
    send[...] = jnp.broadcast_to((jnp.sum(got[...], axis=0) * scale)[None], send.shape)


def split_kernel(got, left, right, gate, out):
    for t, (ref, lane) in enumerate(
        ((left, 0), (left, 128), (right, 0), (right, 128), (gate, 0), (out, 0))
    ):
        for half in range(2):
            ref[half * 64 : (half + 1) * 64, lane : lane + 128] = got[
                pl.ds(2 * t + half, 64, stride=16), :
            ]


def call(kernel, grid, in_specs, out_specs, out_shape, scratch=(), cost=(10**9, 10**7)):
    return pl.pallas_call(
        kernel,
        grid=grid,
        in_specs=in_specs,
        out_specs=out_specs,
        out_shape=out_shape,
        scratch_shapes=list(scratch),
        cost_estimate=pl.CostEstimate(flops=cost[0], bytes_accessed=cost[1], transcendentals=0),
        compiler_params=pltpu.CompilerParams(vmem_limit_bytes=48 * 1024 * 1024),
    )


def whole(*shape):
    return pl.BlockSpec(shape, lambda *_: (0,) * len(shape))


def shape(dims, kind):
    return jax.ShapeDtypeStruct(dims, kind)


def exchange(values):
    return lax.all_to_all(values, AXES, 0, 0, tiled=True)


def body(
    pair, length, ln_in_gain, ln_in_bias, w_left, w_right, w_gate,
    product_norm_gain, product_norm_bias, w_out, cotangent,
):
    tile_i, tile_j, chans = pair.shape
    total = tile_j * lax.axis_size("col")
    steps = tile_i // STEP
    cells = tile_i * tile_j
    grid = (steps,)
    gain_in, bias_in = ln_in_gain.reshape(1, 128), ln_in_bias.reshape(1, 128)
    gain_p, bias_p = product_norm_gain.reshape(1, 128), product_norm_bias.reshape(1, 128)

    natural = pl.BlockSpec((STEP, 64, 128), lambda i: (i, 0, 0))
    chan_major = pl.BlockSpec((128, STEP * 64), lambda i: (0, i))
    chan_major2 = pl.BlockSpec((256, STEP * 64), lambda i: (0, i))
    single = pl.BlockSpec((64, STEP, 128), lambda i: (0, i, 0))
    double = pl.BlockSpec((64, 2, STEP, 128), lambda i: (0, 0, i, 0))
    scalar = pl.BlockSpec(memory_space=pltpu.SMEM)
    vec, wide, square = whole(1, 128), whole(128, 256), whole(128, 128)
    swap = pltpu.VMEM((64 * STEP, 128), F32)
    f_cells, b_cells = shape((128, cells), F32), shape((128, cells), BF)

    send, zn = call(
        operands_kernel, grid,
        [natural, scalar, vec, vec, wide, wide],
        [double, chan_major],
        [shape((64, 2, 64, 128), BF), b_cells],
        [swap],
    )(pair, length, gain_in, bias_in, w_left, w_right)
    operands = exchange(send.reshape(64, 128, 128)).reshape(64, 2, 64, 128)

    slope_l, bend_l, slope_r, bend_r, gate, upstream = call(
        factors_kernel, grid,
        [chan_major, scalar, wide, wide, square, natural],
        [chan_major] * 6,
        [f_cells] * 6,
    )(zn, length, w_left, w_right, w_gate, cotangent)

    product = call(
        product_kernel, (1,),
        [whole(64, 2, 64, 128)],
        whole(64, 64, 128),
        shape((64, 64, 128), BF),
        [pltpu.VMEM((512, 1024), BF), pltpu.VMEM((1024, 1024), BF)],
    )(operands)

    updated, send, d_gpre, grad_out, grad_gate = call(
        middle_kernel, grid,
        [single, chan_major, chan_major, chan_major, vec, vec, square],
        [natural, single, chan_major, square, square],
        [shape(pair.shape, BF), shape((64, 64, 128), BF), b_cells]
        + [shape((128, 128), F32)] * 2,
        [swap],
    )(exchange(product), gate, upstream, zn, gain_p, bias_p, w_out)

    send = call(
        product_grads_kernel, (1,),
        [whole(64, 64, 128), whole(64, 2, 64, 128)],
        whole(64, 2, 64, 128),
        shape((64, 2, 64, 128), BF),
        [pltpu.VMEM((512, 1024), BF), pltpu.VMEM((1024, 1024), BF), pltpu.VMEM((512, 1024), BF)],
    )(exchange(send), operands)
    grads = exchange(send.reshape(64, 128, 128)).reshape(64, 2, 64, 128)

    d_left, d_right, terms = call(
        weights_kernel, grid,
        [double] + [chan_major] * 5 + [square] * 2,
        [chan_major2, chan_major2, whole(1024, 128)],
        [shape((256, cells), BF)] * 2 + [shape((1024, 128), F32)],
        [swap, pltpu.VMEM((128, 512), F32)],
    )(grads, zn, slope_l, bend_l, slope_r, bend_r, grad_gate, grad_out)
    shares = exchange(terms.reshape(64, 16, 128))

    d_pair = call(
        pair_kernel, grid,
        [natural, vec, chan_major2, chan_major2, chan_major, wide, wide, square],
        natural,
        shape(pair.shape, BF),
    )(pair, gain_in, d_left, d_right, d_gpre, w_left, w_right, w_gate)

    summed = call(
        functools.partial(sum_kernel, 1.0 / total), (1,),
        [whole(64, 16, 128)], whole(64, 16, 128), shape((64, 16, 128), F32), cost=(10**6, 10**6),
    )(shares)
    sums = call(
        split_kernel, (1,),
        [whole(1024, 128)],
        [wide, wide, square, square],
        [shape((128, 256), F32)] * 2 + [shape((128, 128), F32)] * 2, cost=(10**6, 10**6),
    )(exchange(summed).reshape(1024, 128))
    return (updated, d_pair, *sums)


def solution(mesh):
    in_specs = (
        P(("rep", "row"), "col", None),
        P("rep"),
        P(),
        P(),
        P(),
        P(),
        P(),
        P(),
        P(),
        P(),
        P(("rep", "row"), "col", None),
    )
    out_specs = (
        P(("rep", "row"), "col", None),
        P(("rep", "row"), "col", None),
        P("rep", None),
        P("rep", None),
        P("rep", None),
        P("rep", None),
    )
    return jax.shard_map(body, mesh=mesh, in_specs=in_specs, out_specs=out_specs, check_vma=False)
```

```python
import functools

import jax
import jax.numpy as jnp
from jax import lax
from jax.experimental import pallas as pl
from jax.experimental.pallas import tpu as pltpu
from jax.sharding import PartitionSpec as P

AXES = ("row", "col")
BF = jnp.bfloat16
F32 = jnp.float32
PAIRS = 16
CHUNK = 8
CELLS = PAIRS * 128
LIMIT = 32 * 1024 * 1024
EPS = 1e-05


def dot(lhs, rhs, left_dim, right_dim):
    return lax.dot_general(
        lhs, rhs, (((left_dim,), (right_dim,)), ((), ())), preferred_element_type=F32
    )


def column(ref):
    return jnp.transpose(jnp.broadcast_to(ref[...], (128, 128)))[:, :1]


def normalize(values):
    centered = values - jnp.mean(values, axis=0, keepdims=True)
    inverse = lax.rsqrt(jnp.mean(centered * centered, axis=0, keepdims=True) + EPS)
    return centered * inverse, inverse


def normalize_backward(grad_hat, normed, inverse):
    return inverse * (
        grad_hat
        - jnp.mean(grad_hat, axis=0, keepdims=True)
        - normed * jnp.mean(grad_hat * normed, axis=0, keepdims=True)
    )


def spans():
    return [(p, p * 128) for p in range(0, PAIRS, CHUNK)]


def load_transposed(ref, first):
    rows = [ref[half, first + p] for p in range(CHUNK) for half in range(2)]
    return jnp.transpose(jnp.concatenate(rows, axis=0)).astype(F32)


def store_transposed(ref, first, values):
    rows = jnp.transpose(values.astype(BF))
    for p in range(CHUNK):
        for half in range(2):
            start = (2 * p + half) * 64
            ref[half, first + p] = rows[start : start + 64]


def lanes(cell):
    return slice(cell, cell + CHUNK * 128)


def low_half(dims):
    return lax.broadcasted_iota(jnp.int32, dims, len(dims) - 1) < 64


def pack(values, first, scr):
    for p in range(CHUNK):
        scr[pl.ds(first + p, 64, stride=PAIRS), :] = values[:, p * 128 : (p + 1) * 128]


def packed(scr):
    return scr[...].reshape(64, PAIRS, 128).astype(BF)


def spread(payload, scr):
    scr[...] = payload.astype(F32).reshape(64 * PAIRS, 128)


def unpack(scr, first):
    return jnp.concatenate(
        [scr[pl.ds(first + p, 64, stride=PAIRS), :] for p in range(CHUNK)], axis=1
    )


def cell_mask(length_ref, first):
    cells = lax.broadcasted_iota(jnp.int32, (1, CHUNK * 128), 1)
    pair = pl.program_id(0) * PAIRS + first + cells // 128
    row = lax.axis_index("row") * 64 + pair + 32 * ((cells // 64) % 2)
    col = lax.axis_index("col") * 64 + cells % 64
    length = length_ref[0]
    return ((row < length) & (col < length)).astype(F32)


def half_weights(ref_left, ref_right, half):
    parts = []
    for ref in (ref_left, ref_right):
        turned = jnp.transpose(ref[...])
        for start in (half * 64, 128 + half * 64):
            parts.append(turned[start : start + 64])
    return jnp.concatenate(parts, axis=0)


def operands_kernel(
    pair, length, gain_ref, bias_ref, w_left, w_right, send, zn_out, *scratch
):
    gain, bias = column(gain_ref), column(bias_ref)
    weights = [half_weights(w_left, w_right, half) for half in range(2)]
    for first, cell in spans():
        zhat, _ = normalize(load_transposed(pair, first))
        zn = (zhat * gain + bias).astype(BF)
        zn_out[:, lanes(cell)] = zn
        mask = cell_mask(length, first)
        for half in range(2):
            both = dot(weights[half], zn, 1, 0)
            for which in range(2):
                value = both[which * 128 : which * 128 + 64]
                sigma = jax.nn.sigmoid(both[which * 128 + 64 : which * 128 + 128])
                pack(mask * sigma * value, first, scratch[2 * half + which])
    for half in range(2):
        for which in range(2):
            send[:, 2 * half + which] = packed(scratch[2 * half + which])


def factors_kernel(
    zn_ref, length, cot, gain_ref, w_left, w_right, w_gate, w_out, sl, gl, sr, gr, hat_grad
):
    gain = column(gain_ref)
    for first, cell in spans():
        here = lanes(cell)
        zn = zn_ref[:, here]
        mask = cell_mask(length, first)
        gate = jax.nn.sigmoid(dot(w_gate[...], zn, 0, 0))
        d_proj = (load_transposed(cot, first) * gate).astype(BF)
        hat_grad[:, here] = dot(w_out[...], d_proj, 1, 0) * gain
        for weights, slope, bend in ((w_left, sl, gl), (w_right, sr, gr)):
            value = dot(weights[...], zn, 0, 0)
            sigma = jax.nn.sigmoid(value[128:])
            slope[:, here] = (mask * sigma).astype(BF)
            bend[:, here] = (mask * value[:128] * sigma * (1.0 - sigma)).astype(BF)


def tile_lanes(col):
    return slice(col * 128, (col + 1) * 128)


def gather_map(got, which, scr):
    for r in range(8):
        for c in range(8):
            scr[r * 32 : (r + 1) * 32, tile_lanes(c)] = got[r * 8 + c, which]


def spread_rows(got, which, scr):
    low = low_half((32, 128))
    for r in range(8):
        for c in range(8):
            tile = got[r * 8 + c, which].astype(F32)
            turned = pltpu.roll(tile, 64, 1)
            blocks = (
                jnp.where(low, tile, 0.0),
                jnp.where(low, turned, 0.0),
                jnp.where(low, 0.0, turned),
                jnp.where(low, 0.0, tile),
            )
            scr[r * 128 : (r + 1) * 128, tile_lanes(c)] = jnp.concatenate(blocks, axis=0).astype(BF)


def product_kernel(got, send, a_scr, b_scr):
    for half in range(2):
        gather_map(got, 2 * half, a_scr)
        spread_rows(got, 2 * half + 1, b_scr)
        for n in range(4):
            out = dot(a_scr[...], b_scr[n * 256 : (n + 1) * 256, :], 1, 1).astype(BF)
            for r in range(8):
                for c in range(2):
                    send[r * 8 + 2 * n + c, half] = out[r * 32 : (r + 1) * 32, tile_lanes(c)]


def middle_kernel(
    got, hat_grad, gain_ref, bias_ref, send, y_out, scr_0, scr_1, out_0, out_1
):
    spread(got[:, 0], scr_0)
    spread(got[:, 1], scr_1)
    gain, bias = column(gain_ref), column(bias_ref)
    for first, cell in spans():
        here = lanes(cell)
        values = jnp.concatenate([unpack(scr_0, first), unpack(scr_1, first)], axis=0)
        hat, inverse = normalize(values)
        d_prod = normalize_backward(hat_grad[:, here], hat, inverse)
        pack(d_prod[:64], first, out_0)
        pack(d_prod[64:], first, out_1)
        y_out[:, here] = (hat * gain + bias).astype(BF)
    send[:, 0] = packed(out_0)
    send[:, 1] = packed(out_1)


def updated_kernel(y_ref, zn_ref, cot, w_out, w_gate, updated, dg_out, grad_out, grad_gate):
    @pl.when(pl.program_id(0) == 0)
    def _():
        grad_out[...] = jnp.zeros((128, 128), F32)
        grad_gate[...] = jnp.zeros((128, 128), F32)

    for first, cell in spans():
        here = lanes(cell)
        y, zn = y_ref[:, here], zn_ref[:, here]
        gate = jax.nn.sigmoid(dot(w_gate[...], zn, 0, 0))
        upstream = load_transposed(cot, first)
        proj = dot(w_out[...], y, 0, 0)
        d_proj = (upstream * gate).astype(BF)
        d_gpre = (upstream * proj * gate * (1.0 - gate)).astype(BF)
        store_transposed(updated, first, gate * proj)
        dg_out[:, here] = d_gpre
        grad_out[...] += dot(y, d_proj, 1, 1)
        grad_gate[...] += dot(zn, d_gpre, 1, 1)


def product_grads_kernel(got, operands_ref, send, a_scr, b_scr, d_scr):
    low = low_half((32, 128))
    for half in range(2):
        gather_map(operands_ref, 2 * half, a_scr)
        spread_rows(operands_ref, 2 * half + 1, b_scr)
        gather_map(got, half, d_scr)
        for n in range(4):
            out = dot(d_scr[...], b_scr[:, n * 256 : (n + 1) * 256], 1, 0).astype(BF)
            for r in range(8):
                for c in range(2):
                    send[r * 8 + 2 * n + c, 2 * half] = out[r * 32 : (r + 1) * 32, tile_lanes(c)]
        for m in range(2):
            out = dot(d_scr[:, m * 512 : (m + 1) * 512], a_scr[...], 0, 0)
            for r in range(4):
                for c in range(8):
                    block = out[r * 128 : (r + 1) * 128, tile_lanes(c)]
                    same = jnp.where(low, block[:32], block[96:])
                    cross = jnp.where(low, block[32:64], block[64:96])
                    send[(m * 4 + r) * 8 + c, 2 * half + 1] = (
                        same + pltpu.roll(cross, 64, 1)
                    ).astype(BF)


def weights_kernel(
    got, zn, sl, gl, sr, gr, grad_gate, grad_out, dl_out, dr_out, send, acc, stage, scr_0, scr_1
):
    @pl.when(pl.program_id(0) == 0)
    def _():
        acc[...] = jnp.zeros((128, 512), F32)

    for which, slope, bend, out in ((0, sl, gl, dl_out), (1, sr, gr, dr_out)):
        spread(got[:, which], scr_0)
        spread(got[:, 2 + which], scr_1)
        for first, cell in spans():
            here = lanes(cell)
            grad = jnp.concatenate([unpack(scr_0, first), unpack(scr_1, first)], axis=0)
            value = jnp.concatenate(
                [grad * slope[:, here], grad * bend[:, here]], axis=0
            ).astype(BF)
            out[:, here] = value
            acc[:, which * 256 : (which + 1) * 256] += dot(zn[:, here], value, 1, 1)

    @pl.when(pl.program_id(0) == pl.num_programs(0) - 1)
    def _():
        for t in range(6):
            if t < 4:
                tile = acc[:, tile_lanes(t)]
            else:
                tile = (grad_gate if t == 4 else grad_out)[...]
            for half in range(2):
                stage[pl.ds(2 * t + half, 64, stride=16), :] = tile[half * 64 : (half + 1) * 64]
        for t in range(12, 16):
            stage[pl.ds(t, 64, stride=16), :] = jnp.zeros((64, 128), F32)
        send[...] = stage[...].reshape(64, 16, 128).astype(BF)


def pair_kernel(pair, gain_ref, dl, dr, dg, w_left, w_right, w_gate, out):
    gain = column(gain_ref)
    for first, cell in spans():
        here = lanes(cell)
        zhat, inverse = normalize(load_transposed(pair, first))
        d_zn = (
            dot(w_left[...], dl[:, here], 1, 0)
            + dot(w_right[...], dr[:, here], 1, 0)
            + dot(w_gate[...], dg[:, here], 1, 0)
        )
        store_transposed(out, first, normalize_backward(d_zn * gain, zhat, inverse))


def sum_kernel(scale, got, send):
    total = got[0].astype(F32)
    for s in range(1, 64):
        total = total + got[s].astype(F32)
    send[...] = jnp.broadcast_to((total * scale).astype(BF)[None], send.shape)


def split_kernel(got, left, right, gate, out, stage):
    stage[...] = got[...].astype(F32).reshape(1024, 128)
    for t, (ref, lane) in enumerate(
        ((left, 0), (left, 128), (right, 0), (right, 128), (gate, 0), (out, 0))
    ):
        for half in range(2):
            ref[half * 64 : (half + 1) * 64, lane : lane + 128] = stage[
                pl.ds(2 * t + half, 64, stride=16), :
            ]


def call(kernel, grid, in_specs, out_specs, out_shape, scratch=(), cost=(10**9, 10**7)):
    return pl.pallas_call(
        kernel,
        grid=grid,
        in_specs=in_specs,
        out_specs=out_specs,
        out_shape=out_shape,
        scratch_shapes=list(scratch),
        cost_estimate=pl.CostEstimate(flops=cost[0], bytes_accessed=cost[1], transcendentals=0),
        compiler_params=pltpu.CompilerParams(vmem_limit_bytes=LIMIT),
    )


def whole(*dims):
    return pl.BlockSpec(dims, lambda *_: (0,) * len(dims))


def shape(dims, kind, space=None):
    return jax.ShapeDtypeStruct(dims, kind) if space is None else space(dims, kind)


def keep(value, space):
    return pltpu.with_memory_space_constraint(value, space)


def exchange(values):
    owners = values.shape[0]
    flat = values.reshape(owners, -1, 128)
    return lax.all_to_all(flat, AXES, 0, 0, tiled=True).reshape(values.shape)


def body(
    pair, length, ln_in_gain, ln_in_bias, w_left, w_right, w_gate,
    product_norm_gain, product_norm_bias, w_out, cotangent,
):
    tile_i, tile_j, chans = pair.shape
    total = tile_j * lax.axis_size("col")
    cells = tile_i * tile_j
    grid = (32 // PAIRS,)
    gain_in, bias_in = ln_in_gain.reshape(1, 128), ln_in_bias.reshape(1, 128)
    gain_p, bias_p = product_norm_gain.reshape(1, 128), product_norm_bias.reshape(1, 128)
    halves = (2, tile_i // 2, tile_j, chans)
    pair = keep(pair.reshape(halves), pltpu.HBM)
    cotangent = keep(cotangent.reshape(halves), pltpu.HBM)
    w_left, w_right, w_gate, w_out = (
        keep(w, pltpu.HBM) for w in (w_left, w_right, w_gate, w_out)
    )

    natural = pl.BlockSpec((2, PAIRS, 64, 128), lambda i: (0, i, 0, 0))
    chan_major = pl.BlockSpec((128, CELLS), lambda i: (0, i))
    chan_major2 = pl.BlockSpec((256, CELLS), lambda i: (0, i))
    double = pl.BlockSpec((64, 2, PAIRS, 128), lambda i: (0, 0, i, 0))
    quad = pl.BlockSpec((64, 4, PAIRS, 128), lambda i: (0, 0, i, 0))
    scalar = pl.BlockSpec(memory_space=pltpu.SMEM)
    vec, wide, square = whole(1, 128), whole(128, 256), whole(128, 128)
    swap = pltpu.VMEM((64 * PAIRS, 128), F32)
    near, far = pltpu.VMEM, pltpu.HBM
    b_cells = shape((128, cells), BF, far)
    pay2, pay4 = shape((64, 2, 32, 128), BF, far), shape((64, 4, 32, 128), BF, far)
    f_square = shape((128, 128), F32, far)
    a_map, b_map = pltpu.VMEM((256, 1024), BF), pltpu.VMEM((1024, 1024), BF)

    send, zn = call(
        operands_kernel, grid,
        [natural, scalar, vec, vec, wide, wide],
        [quad, chan_major],
        [pay4, b_cells],
        [swap] * 4,
    )(pair, length, gain_in, bias_in, w_left, w_right)
    zn = keep(zn, far)
    operands = exchange(send)

    *factors, hat_grad = call(
        factors_kernel, grid,
        [chan_major, scalar, natural, vec, wide, wide, square, square],
        [chan_major] * 5,
        [b_cells] * 4 + [shape((128, cells), F32, far)],
    )(zn, length, cotangent, gain_p, w_left, w_right, w_gate, w_out)
    factors = [keep(f, far) for f in factors]

    product = call(
        product_kernel, (1,), [whole(64, 4, 32, 128)], whole(64, 2, 32, 128), pay2, [a_map, b_map]
    )(keep(operands, near))

    send, y = call(
        middle_kernel, grid,
        [double, chan_major, vec, vec],
        [double, chan_major],
        [pay2, b_cells],
        [swap] * 4,
    )(keep(exchange(product), near), keep(hat_grad, far), gain_p, bias_p)
    got = exchange(send)

    updated, d_gpre, grad_out, grad_gate = call(
        updated_kernel, grid,
        [chan_major, chan_major, natural, square, square],
        [natural, chan_major, square, square],
        [shape(halves, BF, far), b_cells, f_square, f_square],
    )(keep(y, far), zn, cotangent, w_out, w_gate)

    send = call(
        product_grads_kernel, (1,),
        [whole(64, 2, 32, 128), whole(64, 4, 32, 128)],
        whole(64, 4, 32, 128),
        pay4,
        [a_map, b_map, a_map],
    )(keep(got, near), keep(operands, near))

    d_left, d_right, terms = call(
        weights_kernel, grid,
        [quad] + [chan_major] * 5 + [square, square],
        [chan_major2, chan_major2, whole(64, 16, 128)],
        [shape((256, cells), BF, far)] * 2 + [shape((64, 16, 128), BF, far)],
        [pltpu.VMEM((128, 512), F32), pltpu.VMEM((1024, 128), F32), swap, swap],
    )(keep(exchange(send), near), zn, *factors, keep(grad_gate, far), keep(grad_out, far))
    shares = exchange(terms)

    d_pair = call(
        pair_kernel, grid,
        [natural, vec, chan_major2, chan_major2, chan_major, wide, wide, square],
        natural,
        shape(halves, BF, far),
    )(pair, gain_in, keep(d_left, far), keep(d_right, far), keep(d_gpre, far), w_left, w_right, w_gate)

    summed = call(
        functools.partial(sum_kernel, 1.0 / total), (1,),
        [whole(64, 16, 128)], whole(64, 16, 128), shape((64, 16, 128), BF, far), cost=(10**6, 10**6),
    )(shares)
    sums = call(
        split_kernel, (1,),
        [whole(64, 16, 128)],
        [wide, wide, square, square],
        [shape((128, 256), F32)] * 2 + [shape((128, 128), F32)] * 2,
        [pltpu.VMEM((1024, 128), F32)],
        cost=(10**6, 10**6),
    )(exchange(summed))
    full = (tile_i, tile_j, chans)
    return (updated.reshape(full), d_pair.reshape(full), *sums)


def solution(mesh):
    in_specs = (
        P(("rep", "row"), "col", None),
        P("rep"),
        P(),
        P(),
        P(),
        P(),
        P(),
        P(),
        P(),
        P(),
        P(("rep", "row"), "col", None),
    )
    out_specs = (
        P(("rep", "row"), "col", None),
        P(("rep", "row"), "col", None),
        P("rep", None),
        P("rep", None),
        P("rep", None),
        P("rep", None),
    )
    return jax.shard_map(body, mesh=mesh, in_specs=in_specs, out_specs=out_specs, check_vma=False)
```

```python
import functools

import jax
import jax.numpy as jnp
from jax import lax
from jax.experimental import pallas as pl
from jax.experimental.pallas import tpu as pltpu
from jax.sharding import PartitionSpec as P

AXES = ("row", "col")
BF = jnp.bfloat16
F32 = jnp.float32
STEP = 16
ROWS = 16
PITCH = 17
CELLS = STEP * 64
LIMIT = 32 * 1024 * 1024
EPS = 1e-05


def dot(lhs, rhs, left_dim, right_dim):
    return lax.dot_general(
        lhs, rhs, (((left_dim,), (right_dim,)), ((), ())), preferred_element_type=F32
    )


def column(ref):
    return jnp.transpose(jnp.broadcast_to(ref[...], (128, 128)))[:, :1]


def normalize(values):
    centered = values - jnp.mean(values, axis=0, keepdims=True)
    inverse = lax.rsqrt(jnp.mean(centered * centered, axis=0, keepdims=True) + EPS)
    return centered * inverse, inverse


def normalize_backward(grad_hat, normed, inverse):
    return inverse * (
        grad_hat
        - jnp.mean(grad_hat, axis=0, keepdims=True)
        - normed * jnp.mean(grad_hat * normed, axis=0, keepdims=True)
    )


def sigmoid(values):
    return 0.5 * jnp.tanh(0.5 * values) + 0.5


def spans(rows):
    return [(i, slice(i * 64, (i + rows) * 64)) for i in range(0, STEP, rows)]


def load_transposed(ref, first, rows):
    return jnp.transpose(ref[first : first + rows].reshape(rows * 64, 128)).astype(F32)


def store_transposed(ref, first, values):
    rows = values.shape[1] // 64
    ref[first : first + rows] = jnp.transpose(values.astype(BF)).reshape(rows, 64, 128)


def low_half(dims):
    return lax.broadcasted_iota(jnp.int32, dims, len(dims) - 1) < 64


def pack(values, first, scr):
    low = low_half((64, 128))
    for t in range(values.shape[1] // 128):
        lane = slice(t * 128, (t + 1) * 128)
        upper, lower = values[:64, lane], values[64:, lane]
        row = first + 2 * t
        scr[pl.ds(row, 64, stride=PITCH), :] = jnp.where(low, upper, pltpu.roll(lower, 64, 1))
        scr[pl.ds(row + 1, 64, stride=PITCH), :] = jnp.where(low, pltpu.roll(upper, 64, 1), lower)


def packed(scr, kind=BF):
    return jnp.stack([scr[d * PITCH : d * PITCH + STEP] for d in range(64)]).astype(kind)


def spread(payload, scr):
    wide = payload.astype(F32)
    for d in range(64):
        scr[d * PITCH : d * PITCH + STEP] = wide[d]


def unpack(scr, first, rows):
    low = low_half((64, 128))
    tiles = []
    for row in range(first, first + rows, 2):
        even = scr[pl.ds(row, 64, stride=PITCH), :]
        odd = scr[pl.ds(row + 1, 64, stride=PITCH), :]
        upper = jnp.where(low, even, pltpu.roll(odd, 64, 1))
        lower = jnp.where(low, pltpu.roll(even, 64, 1), odd)
        tiles.append(jnp.concatenate([upper, lower], axis=0))
    return jnp.concatenate(tiles, axis=1) if len(tiles) > 1 else tiles[0]


def cell_mask(length_ref, first, rows):
    cells = lax.broadcasted_iota(jnp.int32, (1, rows * 64), 1)
    row = lax.axis_index("row") * 64 + pl.program_id(0) * STEP + first + cells // 64
    col = lax.axis_index("col") * 64 + cells % 64
    length = length_ref[0]
    return ((row < length) & (col < length)).astype(F32)


def operands_kernel(pair, length, gain_ref, bias_ref, w_left, w_right, send, zn_out, scr_a, scr_b):
    gain, bias = column(gain_ref), column(bias_ref)
    weights = [jnp.transpose(ref[...]) for ref in (w_left, w_right)]
    for first, here in spans(ROWS):
        zhat, _ = normalize(load_transposed(pair, first, ROWS))
        zn = (zhat * gain + bias).astype(BF)
        zn_out[:, here] = zn
        mask = cell_mask(length, first, ROWS)
        for weight, scr in zip(weights, (scr_a, scr_b)):
            both = dot(weight, zn, 1, 0)
            pack(mask * sigmoid(both[128:]) * both[:128], first, scr)
    rows = pl.ds(pl.multiple_of(pl.program_id(0) * STEP, STEP), STEP)
    send[:, 0, rows] = packed(scr_a)
    send[:, 1, rows] = packed(scr_b)


def factors_kernel(
    zn_ref, length, cot, gain_ref, w_left, w_right, w_gate, w_out,
    sl, gl, sr, gr, hat_grad, zn_cells, scr,
):
    gain = column(gain_ref)
    for first, here in spans(ROWS):
        zn = zn_ref[:, here]
        zn_cells[here] = jnp.transpose(zn)
        mask = cell_mask(length, first, ROWS)
        gate = sigmoid(dot(w_gate[...], zn, 0, 0))
        d_proj = (load_transposed(cot, first, ROWS) * gate).astype(BF)
        pack(dot(w_out[...], d_proj, 1, 0) * gain, first, scr)
        for weights, slope, bend in ((w_left, sl, gl), (w_right, sr, gr)):
            value = dot(weights[...], zn, 0, 0)
            sigma = sigmoid(value[128:])
            slope[:, here] = (mask * sigma).astype(BF)
            bend[:, here] = (mask * value[:128] * sigma * (1.0 - sigma)).astype(BF)
    hat_grad[...] = packed(scr, F32)


def gather_map(got, which, scr):
    for r in range(8):
        for c in range(8):
            scr[r * 64 : (r + 1) * 64, c * 128 : (c + 1) * 128] = got[r * 8 + c, which]


def double_rows(got, which, scr):
    low = low_half((64, 128))
    zero = jnp.zeros((64, 128), BF)
    for r in range(8):
        for c in range(8):
            tile = got[r * 8 + c, which]
            lanes = slice(c * 128, (c + 1) * 128)
            scr[r * 128 : r * 128 + 64, lanes] = jnp.where(low, tile, zero)
            scr[r * 128 + 64 : (r + 1) * 128, lanes] = jnp.where(low, zero, tile)


def product_kernel(got, send, a_scr, b_scr, out_scr, sems):
    gather_map(got, 0, a_scr)
    double_rows(got, 1, b_scr)
    copies = []
    for n in range(4):
        out = dot(a_scr[...], b_scr[n * 256 : (n + 1) * 256, :], 1, 1).astype(BF)
        for r in range(8):
            for c in range(2):
                out_scr[r, 2 * n + c] = out[r * 64 : (r + 1) * 64, c * 128 : (c + 1) * 128]
        part = (slice(None), pl.ds(2 * n, 2))
        copies.append(pltpu.make_async_copy(out_scr.at[part], send.at[part], sems.at[n]))
        copies[-1].start()
    for copy in copies:
        copy.wait()


def halves_sum(values):
    return values + pltpu.roll(values, 64, 1)


def middle_kernel(got, hat_grad, send):
    rows = pl.ds(pl.multiple_of(pl.program_id(0) * STEP, STEP), STEP)

    def value(d):
        return got[d, rows].astype(F32)

    def channel_mean(term):
        sums = [term(d) for d in range(4)]
        for d in range(4, 64):
            sums[d % 4] = sums[d % 4] + term(d)
        return halves_sum((sums[0] + sums[1]) + (sums[2] + sums[3])) * (1.0 / 128)

    mean = channel_mean(value)
    inverse = lax.rsqrt(channel_mean(lambda d: (value(d) - mean) * (value(d) - mean)) + EPS)
    first = channel_mean(lambda d: hat_grad[d])
    second = channel_mean(lambda d: hat_grad[d] * ((value(d) - mean) * inverse))
    for d in range(64):
        hat = (value(d) - mean) * inverse
        send[d, rows] = (inverse * (hat_grad[d] - first - hat * second)).astype(BF)


def updated_kernel(
    product, zn_ref, cot, gain_ref, bias_ref, w_out, w_gate,
    updated, dg_out, grad_out, grad_gate, scr,
):
    @pl.when(pl.program_id(0) == 0)
    def _():
        grad_out[...] = jnp.zeros((128, 128), F32)
        grad_gate[...] = jnp.zeros((128, 128), F32)

    spread(product[...], scr)
    gain, bias = column(gain_ref), column(bias_ref)
    for first, here in spans(ROWS):
        hat, _ = normalize(unpack(scr, first, ROWS))
        y = (hat * gain + bias).astype(BF)
        zn = zn_ref[:, here]
        gate = sigmoid(dot(w_gate[...], zn, 0, 0))
        upstream = load_transposed(cot, first, ROWS)
        proj = dot(w_out[...], y, 0, 0)
        d_proj = (upstream * gate).astype(BF)
        d_gpre = (upstream * proj * gate * (1.0 - gate)).astype(BF)
        store_transposed(updated, first, gate * proj)
        dg_out[:, here] = d_gpre
        grad_out[...] += dot(y, d_proj, 1, 1)
        grad_gate[...] += dot(zn, d_gpre, 1, 1)


def product_grads_kernel(got, operands_ref, send, a_scr, b_scr, d_scr):
    gather_map(operands_ref, 0, a_scr)
    double_rows(operands_ref, 1, b_scr)
    for r in range(8):
        for c in range(8):
            d_scr[r * 64 : (r + 1) * 64, c * 128 : (c + 1) * 128] = got[r * 8 + c]
    for n in range(4):
        out = dot(d_scr[...], b_scr[:, n * 256 : (n + 1) * 256], 1, 0).astype(BF)
        for r in range(8):
            for c in range(2):
                send[r * 8 + 2 * n + c, 0] = out[r * 64 : (r + 1) * 64, c * 128 : (c + 1) * 128]
    low = low_half((64, 128))
    for m in range(2):
        out = dot(d_scr[:, m * 512 : (m + 1) * 512], a_scr[...], 0, 0)
        for r in range(4):
            for c in range(8):
                lanes = slice(c * 128, (c + 1) * 128)
                send[(m * 4 + r) * 8 + c, 1] = jnp.where(
                    low, out[r * 128 : r * 128 + 64, lanes], out[r * 128 + 64 : (r + 1) * 128, lanes]
                ).astype(BF)


def weights_kernel(
    got, zn_cells, sl, gl, sr, gr, grad_gate, grad_out, dl_out, dr_out, send, acc, stage, scr
):
    @pl.when(pl.program_id(0) == 0)
    def _():
        acc[...] = jnp.zeros((512, 128), F32)

    rows = pl.ds(pl.multiple_of(pl.program_id(0) * STEP, STEP), STEP)
    for which, slope, bend, out in ((0, sl, gl, dl_out), (1, sr, gr, dr_out)):
        spread(got[:, which, rows], scr)
        grad = unpack(scr, 0, STEP)
        out[:128] = (grad * slope[...]).astype(BF)
        out[128:] = (grad * bend[...]).astype(BF)
        acc[which * 256 : (which + 1) * 256] += dot(out[...], zn_cells[...], 1, 0)

    @pl.when(pl.program_id(0) == pl.num_programs(0) - 1)
    def _():
        for t in range(6):
            if t < 4:
                tile = acc[t * 128 : (t + 1) * 128]
            else:
                tile = (grad_gate if t == 4 else grad_out)[...]
            for half in range(2):
                stage[pl.ds(2 * t + half, 64, stride=16), :] = tile[half * 64 : (half + 1) * 64]
        for t in range(12, 16):
            stage[pl.ds(t, 64, stride=16), :] = jnp.zeros((64, 128), F32)
        send[...] = stage[...].reshape(64, 16, 128).astype(BF)


def pair_kernel(pair, gain_ref, dl, dr, dg, w_left, w_right, w_gate, out):
    gain = column(gain_ref)
    for first, here in spans(ROWS):
        zhat, inverse = normalize(load_transposed(pair, first, ROWS))
        d_zn = (
            dot(w_left[...], dl[:, here], 1, 0)
            + dot(w_right[...], dr[:, here], 1, 0)
            + dot(w_gate[...], dg[:, here], 1, 0)
        )
        store_transposed(out, first, normalize_backward(d_zn * gain, zhat, inverse))


def sum_kernel(scale, got, send):
    total = got[0].astype(F32)
    for s in range(1, 64):
        total = total + got[s].astype(F32)
    send[...] = jnp.broadcast_to((total * scale).astype(BF)[None], send.shape)


def split_kernel(got, left, right, gate, out, stage):
    stage[...] = got[...].astype(F32).reshape(1024, 128)
    for t, (ref, lane) in enumerate(
        ((left, 0), (left, 128), (right, 0), (right, 128), (gate, 0), (out, 0))
    ):
        tile = jnp.concatenate(
            [stage[pl.ds(2 * t + half, 64, stride=16), :] for half in range(2)], axis=0
        )
        ref[:, lane : lane + 128] = jnp.transpose(tile) if t < 4 else tile


def call(kernel, grid, in_specs, out_specs, out_shape, scratch=(), cost=(10**9, 10**7)):
    return pl.pallas_call(
        kernel,
        grid=grid,
        in_specs=in_specs,
        out_specs=out_specs,
        out_shape=out_shape,
        scratch_shapes=list(scratch),
        cost_estimate=pl.CostEstimate(flops=cost[0], bytes_accessed=cost[1], transcendentals=0),
        compiler_params=pltpu.CompilerParams(vmem_limit_bytes=LIMIT),
    )


def whole(*dims):
    return pl.BlockSpec(dims, lambda *_: (0,) * len(dims))


def shape(dims, kind, space=None):
    return jax.ShapeDtypeStruct(dims, kind) if space is None else space(dims, kind)


def keep(value, space):
    return pltpu.with_memory_space_constraint(value, space)


def exchange(values):
    owners = values.shape[0]
    flat = values.reshape(owners, -1, 128)
    return lax.all_to_all(flat, AXES, 0, 0, tiled=True).reshape(values.shape)


def body(
    pair, length, ln_in_gain, ln_in_bias, w_left, w_right, w_gate,
    product_norm_gain, product_norm_bias, w_out, cotangent,
):
    tile_i, tile_j, chans = pair.shape
    total = tile_j * lax.axis_size("col")
    cells = tile_i * tile_j
    grid = (tile_i // STEP,)
    gain_in, bias_in = ln_in_gain.reshape(1, 128), ln_in_bias.reshape(1, 128)
    gain_p, bias_p = product_norm_gain.reshape(1, 128), product_norm_bias.reshape(1, 128)
    pair, cotangent = keep(pair, pltpu.HBM), keep(cotangent, pltpu.HBM)
    w_left, w_right, w_gate, w_out = (
        keep(w, pltpu.HBM) for w in (w_left, w_right, w_gate, w_out)
    )

    natural = pl.BlockSpec((STEP, 64, 128), lambda i: (i, 0, 0))
    chan_major = pl.BlockSpec((128, CELLS), lambda i: (0, i))
    chan_major2 = pl.BlockSpec((256, CELLS), lambda i: (0, i))
    cell_major = pl.BlockSpec((CELLS, 128), lambda i: (i, 0))
    single = pl.BlockSpec((64, STEP, 128), lambda i: (0, i, 0))
    double = pl.BlockSpec((64, 2, STEP, 128), lambda i: (0, 0, i, 0))
    direct = pl.BlockSpec(memory_space=pltpu.VMEM)
    scalar = pl.BlockSpec(memory_space=pltpu.SMEM)
    vec, wide, square = whole(1, 128), whole(128, 256), whole(128, 128)
    swap = pltpu.VMEM((64 * PITCH, 128), F32)
    near, far = pltpu.VMEM, pltpu.HBM
    b_cells = shape((128, cells), BF, far)
    f_square = shape((128, 128), F32, far)
    a_map, b_map = pltpu.VMEM((512, 1024), BF), pltpu.VMEM((1024, 1024), BF)

    send, zn = call(
        operands_kernel, grid,
        [natural, scalar, vec, vec, wide, wide],
        [direct, chan_major],
        [shape((64, 2, 64, 128), BF, near), b_cells],
        [swap] * 2,
    )(pair, length, gain_in, bias_in, w_left, w_right)
    zn = keep(zn, far)
    operands = keep(exchange(send), near)

    *factors, hat_grad, zn_cells = call(
        factors_kernel, grid,
        [chan_major, scalar, natural, vec, wide, wide, square, square],
        [chan_major] * 4 + [single, cell_major],
        [b_cells] * 4 + [shape((64, 64, 128), F32, far), shape((cells, 128), BF, far)],
        [swap],
    )(zn, length, cotangent, gain_p, w_left, w_right, w_gate, w_out)
    factors = [keep(f, far) for f in factors]

    product = call(
        product_kernel, (1,),
        [direct],
        pl.BlockSpec(memory_space=pltpu.HBM),
        shape((8, 8, 64, 128), BF, far),
        [a_map, b_map, pltpu.VMEM((8, 8, 64, 128), BF), pltpu.SemaphoreType.DMA((4,))],
    )(operands).reshape(64, 64, 128)

    product = keep(exchange(product), near)
    send = call(
        middle_kernel, grid,
        [direct, single],
        direct,
        shape((64, 64, 128), BF, near),
    )(product, keep(hat_grad, far))
    got = exchange(send)

    updated, d_gpre, grad_out, grad_gate = call(
        updated_kernel, grid,
        [single, chan_major, natural, vec, vec, square, square],
        [natural, chan_major, square, square],
        [shape(pair.shape, BF, far), b_cells, f_square, f_square],
        [swap],
    )(product, zn, cotangent, gain_p, bias_p, w_out, w_gate)

    send = call(
        product_grads_kernel, (1,),
        [direct, direct],
        whole(64, 2, 64, 128),
        shape((64, 2, 64, 128), BF, far),
        [a_map, b_map, a_map],
    )(keep(got, near), operands)

    d_left, d_right, terms = call(
        weights_kernel, grid,
        [direct, cell_major] + [chan_major] * 4 + [square, square],
        [chan_major2, chan_major2, whole(64, 16, 128)],
        [shape((256, cells), BF, far)] * 2 + [shape((64, 16, 128), BF, far)],
        [pltpu.VMEM((512, 128), F32), pltpu.VMEM((1024, 128), F32), swap],
    )(keep(exchange(send), near), keep(zn_cells, far), *factors, keep(grad_gate, far), keep(grad_out, far))
    shares = exchange(terms)

    d_pair = call(
        pair_kernel, grid,
        [natural, vec, chan_major2, chan_major2, chan_major, wide, wide, square],
        natural,
        shape(pair.shape, BF, far),
    )(pair, gain_in, keep(d_left, far), keep(d_right, far), keep(d_gpre, far), w_left, w_right, w_gate)

    summed = call(
        functools.partial(sum_kernel, 1.0 / total), (1,),
        [whole(64, 16, 128)], whole(64, 16, 128), shape((64, 16, 128), BF, far), cost=(10**6, 10**6),
    )(shares)
    sums = call(
        split_kernel, (1,),
        [whole(64, 16, 128)],
        [wide, wide, square, square],
        [shape((128, 256), F32)] * 2 + [shape((128, 128), F32)] * 2,
        [pltpu.VMEM((1024, 128), F32)],
        cost=(10**6, 10**6),
    )(exchange(summed))
    return (updated, d_pair, *sums)


def solution(mesh):
    in_specs = (
        P(("rep", "row"), "col", None),
        P("rep"),
        P(),
        P(),
        P(),
        P(),
        P(),
        P(),
        P(),
        P(),
        P(("rep", "row"), "col", None),
    )
    out_specs = (
        P(("rep", "row"), "col", None),
        P(("rep", "row"), "col", None),
        P("rep", None),
        P("rep", None),
        P("rep", None),
        P("rep", None),
    )
    return jax.shard_map(body, mesh=mesh, in_specs=in_specs, out_specs=out_specs, check_vma=False)
```

```python
import functools

import jax
import jax.numpy as jnp
from jax import lax
from jax.experimental import pallas as pl
from jax.experimental.pallas import tpu as pltpu
from jax.sharding import PartitionSpec as P

AXES = ("row", "col")
BF = jnp.bfloat16
F32 = jnp.float32
STEP = 32
ROWS = 16
PITCH = 33
CELLS = STEP * 64
LIMIT = 32 * 1024 * 1024
EPS = 1e-05


def dot(lhs, rhs, left_dim, right_dim):
    return lax.dot_general(
        lhs, rhs, (((left_dim,), (right_dim,)), ((), ())), preferred_element_type=F32
    )


def column(ref):
    return jnp.transpose(jnp.broadcast_to(ref[...], (128, 128)))[:, :1]


def normalize(values):
    centered = values - jnp.mean(values, axis=0, keepdims=True)
    inverse = lax.rsqrt(jnp.mean(centered * centered, axis=0, keepdims=True) + EPS)
    return centered * inverse, inverse


def normalize_backward(grad_hat, normed, inverse):
    return inverse * (
        grad_hat
        - jnp.mean(grad_hat, axis=0, keepdims=True)
        - normed * jnp.mean(grad_hat * normed, axis=0, keepdims=True)
    )


def sigmoid(values):
    return 0.5 * jnp.tanh(0.5 * values) + 0.5


def spans(rows):
    return [(i, slice(i * 64, (i + rows) * 64)) for i in range(0, STEP, rows)]


def load_transposed(ref, first, rows):
    return jnp.transpose(ref[first : first + rows].reshape(rows * 64, 128)).astype(F32)


def store_transposed(ref, first, values):
    rows = values.shape[1] // 64
    ref[first : first + rows] = jnp.transpose(values.astype(BF)).reshape(rows, 64, 128)


def low_half(dims):
    return lax.broadcasted_iota(jnp.int32, dims, len(dims) - 1) < 64


def pack(values, first, scr):
    low = low_half((64, 128))
    for t in range(values.shape[1] // 128):
        lane = slice(t * 128, (t + 1) * 128)
        upper, lower = values[:64, lane], values[64:, lane]
        row = first + 2 * t
        scr[pl.ds(row, 64, stride=PITCH), :] = jnp.where(low, upper, pltpu.roll(lower, 64, 1))
        scr[pl.ds(row + 1, 64, stride=PITCH), :] = jnp.where(low, pltpu.roll(upper, 64, 1), lower)


def packed(scr, kind=BF):
    return jnp.stack([scr[d * PITCH : d * PITCH + STEP] for d in range(64)]).astype(kind)


def spread(payload, scr):
    wide = payload.astype(F32)
    for d in range(64):
        scr[d * PITCH : d * PITCH + STEP] = wide[d]


def unpack(scr, first, rows):
    low = low_half((64, 128))
    tiles = []
    for row in range(first, first + rows, 2):
        even = scr[pl.ds(row, 64, stride=PITCH), :]
        odd = scr[pl.ds(row + 1, 64, stride=PITCH), :]
        upper = jnp.where(low, even, pltpu.roll(odd, 64, 1))
        lower = jnp.where(low, pltpu.roll(even, 64, 1), odd)
        tiles.append(jnp.concatenate([upper, lower], axis=0))
    return jnp.concatenate(tiles, axis=1) if len(tiles) > 1 else tiles[0]


def cell_mask(length_ref, first, rows):
    cells = lax.broadcasted_iota(jnp.int32, (1, rows * 64), 1)
    row = lax.axis_index("row") * 64 + pl.program_id(0) * STEP + first + cells // 64
    col = lax.axis_index("col") * 64 + cells % 64
    length = length_ref[0]
    return ((row < length) & (col < length)).astype(F32)


def operands_kernel(pair, length, gain_ref, bias_ref, w_left, w_right, send, zn_out, scr_a, scr_b):
    gain, bias = column(gain_ref), column(bias_ref)
    weights = [jnp.transpose(ref[...]) for ref in (w_left, w_right)]
    for first, here in spans(ROWS):
        zhat, _ = normalize(load_transposed(pair, first, ROWS))
        zn = (zhat * gain + bias).astype(BF)
        zn_out[:, here] = zn
        mask = cell_mask(length, first, ROWS)
        for weight, scr in zip(weights, (scr_a, scr_b)):
            both = dot(weight, zn, 1, 0)
            pack(mask * sigmoid(both[128:]) * both[:128], first, scr)
    rows = pl.ds(pl.multiple_of(pl.program_id(0) * STEP, STEP), STEP)
    send[:, 0, rows] = packed(scr_a)
    send[:, 1, rows] = packed(scr_b)


def factors_kernel(
    zn_ref, length, cot, gain_ref, w_left, w_right, w_gate, w_out,
    sl, gl, sr, gr, hat_grad, zn_cells, scr,
):
    gain = column(gain_ref)
    for first, here in spans(ROWS):
        zn = zn_ref[:, here]
        zn_cells[here] = jnp.transpose(zn)
        mask = cell_mask(length, first, ROWS)
        gate = sigmoid(dot(w_gate[...], zn, 0, 0))
        d_proj = (load_transposed(cot, first, ROWS) * gate).astype(BF)
        pack(dot(w_out[...], d_proj, 1, 0) * gain, first, scr)
        for weights, slope, bend in ((w_left, sl, gl), (w_right, sr, gr)):
            value = dot(weights[...], zn, 0, 0)
            sigma = sigmoid(value[128:])
            slope[:, here] = (mask * sigma).astype(BF)
            bend[:, here] = (mask * value[:128] * sigma * (1.0 - sigma)).astype(BF)
    hat_grad[...] = packed(scr, F32)


def gather_map(got, which, scr):
    for r in range(8):
        for c in range(8):
            scr[r * 64 : (r + 1) * 64, c * 128 : (c + 1) * 128] = got[r * 8 + c, which]


def double_rows(got, which, scr):
    low = low_half((64, 128))
    zero = jnp.zeros((64, 128), BF)
    for r in range(8):
        for c in range(8):
            tile = got[r * 8 + c, which]
            lanes = slice(c * 128, (c + 1) * 128)
            scr[r * 128 : r * 128 + 64, lanes] = jnp.where(low, tile, zero)
            scr[r * 128 + 64 : (r + 1) * 128, lanes] = jnp.where(low, zero, tile)


def product_kernel(got, send, a_scr, b_scr, out_scr, sems):
    gather_map(got, 0, a_scr)
    double_rows(got, 1, b_scr)
    copies = []
    for n in range(4):
        out = dot(a_scr[...], b_scr[n * 256 : (n + 1) * 256, :], 1, 1).astype(BF)
        for r in range(8):
            for c in range(2):
                out_scr[r, 2 * n + c] = out[r * 64 : (r + 1) * 64, c * 128 : (c + 1) * 128]
        part = (slice(None), pl.ds(2 * n, 2))
        copies.append(pltpu.make_async_copy(out_scr.at[part], send.at[part], sems.at[n]))
        copies[-1].start()
    for copy in copies:
        copy.wait()


def halves_sum(values):
    return values + pltpu.roll(values, 64, 1)


def middle_kernel(got, hat_grad, send):
    rows = pl.ds(pl.multiple_of(pl.program_id(0) * STEP, STEP), STEP)

    def value(d):
        return got[d, rows].astype(F32)

    def channel_mean(term):
        sums = [term(d) for d in range(4)]
        for d in range(4, 64):
            sums[d % 4] = sums[d % 4] + term(d)
        return halves_sum((sums[0] + sums[1]) + (sums[2] + sums[3])) * (1.0 / 128)

    mean = channel_mean(value)
    inverse = lax.rsqrt(channel_mean(lambda d: (value(d) - mean) * (value(d) - mean)) + EPS)
    first = channel_mean(lambda d: hat_grad[d])
    second = channel_mean(lambda d: hat_grad[d] * ((value(d) - mean) * inverse))
    for d in range(64):
        hat = (value(d) - mean) * inverse
        send[d, rows] = (inverse * (hat_grad[d] - first - hat * second)).astype(BF)


def updated_kernel(
    product, zn_ref, cot, gain_ref, bias_ref, w_out, w_gate,
    updated, dg_out, grad_out, grad_gate, scr,
):
    @pl.when(pl.program_id(0) == 0)
    def _():
        grad_out[...] = jnp.zeros((128, 128), F32)
        grad_gate[...] = jnp.zeros((128, 128), F32)

    spread(product[...], scr)
    gain, bias = column(gain_ref), column(bias_ref)
    for first, here in spans(ROWS):
        hat, _ = normalize(unpack(scr, first, ROWS))
        y = (hat * gain + bias).astype(BF)
        zn = zn_ref[:, here]
        gate = sigmoid(dot(w_gate[...], zn, 0, 0))
        upstream = load_transposed(cot, first, ROWS)
        proj = dot(w_out[...], y, 0, 0)
        d_proj = (upstream * gate).astype(BF)
        d_gpre = (upstream * proj * gate * (1.0 - gate)).astype(BF)
        store_transposed(updated, first, gate * proj)
        dg_out[:, here] = d_gpre
        grad_out[...] += dot(y, d_proj, 1, 1)
        grad_gate[...] += dot(zn, d_gpre, 1, 1)


def product_grads_kernel(got, operands_ref, send, a_scr, b_scr, d_scr):
    gather_map(operands_ref, 0, a_scr)
    double_rows(operands_ref, 1, b_scr)
    for r in range(8):
        for c in range(8):
            d_scr[r * 64 : (r + 1) * 64, c * 128 : (c + 1) * 128] = got[r * 8 + c]
    for n in range(4):
        out = dot(d_scr[...], b_scr[:, n * 256 : (n + 1) * 256], 1, 0).astype(BF)
        for r in range(8):
            for c in range(2):
                send[r * 8 + 2 * n + c, 0] = out[r * 64 : (r + 1) * 64, c * 128 : (c + 1) * 128]
    low = low_half((64, 128))
    for m in range(2):
        out = dot(d_scr[:, m * 512 : (m + 1) * 512], a_scr[...], 0, 0)
        for r in range(4):
            for c in range(8):
                lanes = slice(c * 128, (c + 1) * 128)
                send[(m * 4 + r) * 8 + c, 1] = jnp.where(
                    low, out[r * 128 : r * 128 + 64, lanes], out[r * 128 + 64 : (r + 1) * 128, lanes]
                ).astype(BF)


def cell_grads(got, which, slope, bend, scr):
    rows = pl.ds(pl.multiple_of(pl.program_id(0) * STEP, STEP), STEP)
    spread(got[:, which, rows], scr)
    grad = unpack(scr, 0, STEP)
    return jnp.concatenate([grad * slope[...], grad * bend[...]], axis=0).astype(BF)


def weights_kernel(
    got, zn_cells, sl, gl, sr, gr, grad_gate, grad_out, send, acc, stage, scr
):
    @pl.when(pl.program_id(0) == 0)
    def _():
        acc[...] = jnp.zeros((512, 128), F32)

    for which, slope, bend in ((0, sl, gl), (1, sr, gr)):
        grads = cell_grads(got, which, slope, bend, scr)
        acc[which * 256 : (which + 1) * 256] += dot(grads, zn_cells[...], 1, 0)

    @pl.when(pl.program_id(0) == pl.num_programs(0) - 1)
    def _():
        for t in range(6):
            if t < 4:
                tile = acc[t * 128 : (t + 1) * 128]
            else:
                tile = (grad_gate if t == 4 else grad_out)[...]
            for half in range(2):
                stage[pl.ds(2 * t + half, 64, stride=16), :] = tile[half * 64 : (half + 1) * 64]
        for t in range(12, 16):
            stage[pl.ds(t, 64, stride=16), :] = jnp.zeros((64, 128), F32)
        send[...] = stage[...].reshape(64, 16, 128).astype(BF)


def pair_kernel(pair, gain_ref, got, sl, gl, sr, gr, dg, w_left, w_right, w_gate, out, scr):
    gain = column(gain_ref)
    d_left = cell_grads(got, 0, sl, gl, scr)
    d_right = cell_grads(got, 1, sr, gr, scr)
    for first, here in spans(ROWS):
        zhat, inverse = normalize(load_transposed(pair, first, ROWS))
        d_zn = (
            dot(w_left[...], d_left[:, here], 1, 0)
            + dot(w_right[...], d_right[:, here], 1, 0)
            + dot(w_gate[...], dg[:, here], 1, 0)
        )
        store_transposed(out, first, normalize_backward(d_zn * gain, zhat, inverse))


def sum_kernel(scale, got, send):
    total = got[0].astype(F32)
    for s in range(1, 64):
        total = total + got[s].astype(F32)
    send[...] = jnp.broadcast_to((total * scale).astype(BF)[None], send.shape)


def split_kernel(got, left, right, gate, out, stage):
    stage[...] = got[...].astype(F32).reshape(1024, 128)
    for t, (ref, lane) in enumerate(
        ((left, 0), (left, 128), (right, 0), (right, 128), (gate, 0), (out, 0))
    ):
        tile = jnp.concatenate(
            [stage[pl.ds(2 * t + half, 64, stride=16), :] for half in range(2)], axis=0
        )
        ref[:, lane : lane + 128] = jnp.transpose(tile) if t < 4 else tile


def call(kernel, grid, in_specs, out_specs, out_shape, scratch=(), cost=(10**9, 10**7)):
    return pl.pallas_call(
        kernel,
        grid=grid,
        in_specs=in_specs,
        out_specs=out_specs,
        out_shape=out_shape,
        scratch_shapes=list(scratch),
        cost_estimate=pl.CostEstimate(flops=cost[0], bytes_accessed=cost[1], transcendentals=0),
        compiler_params=pltpu.CompilerParams(vmem_limit_bytes=LIMIT),
    )


def whole(*dims):
    return pl.BlockSpec(dims, lambda *_: (0,) * len(dims))


def shape(dims, kind, space=None):
    return jax.ShapeDtypeStruct(dims, kind) if space is None else space(dims, kind)


def keep(value, space):
    return pltpu.with_memory_space_constraint(value, space)


def exchange(values):
    owners = values.shape[0]
    flat = values.reshape(owners, -1, 128)
    return lax.all_to_all(flat, AXES, 0, 0, tiled=True).reshape(values.shape)


def body(
    pair, length, ln_in_gain, ln_in_bias, w_left, w_right, w_gate,
    product_norm_gain, product_norm_bias, w_out, cotangent,
):
    tile_i, tile_j, chans = pair.shape
    total = tile_j * lax.axis_size("col")
    cells = tile_i * tile_j
    grid = (tile_i // STEP,)
    gain_in, bias_in = ln_in_gain.reshape(1, 128), ln_in_bias.reshape(1, 128)
    gain_p, bias_p = product_norm_gain.reshape(1, 128), product_norm_bias.reshape(1, 128)
    pair, cotangent = keep(pair, pltpu.HBM), keep(cotangent, pltpu.HBM)
    w_left, w_right, w_gate, w_out = (
        keep(w, pltpu.HBM) for w in (w_left, w_right, w_gate, w_out)
    )

    natural = pl.BlockSpec((STEP, 64, 128), lambda i: (i, 0, 0))
    chan_major = pl.BlockSpec((128, CELLS), lambda i: (0, i))
    cell_major = pl.BlockSpec((CELLS, 128), lambda i: (i, 0))
    single = pl.BlockSpec((64, STEP, 128), lambda i: (0, i, 0))
    double = pl.BlockSpec((64, 2, STEP, 128), lambda i: (0, 0, i, 0))
    direct = pl.BlockSpec(memory_space=pltpu.VMEM)
    scalar = pl.BlockSpec(memory_space=pltpu.SMEM)
    vec, wide, square = whole(1, 128), whole(128, 256), whole(128, 128)
    swap = pltpu.VMEM((64 * PITCH, 128), F32)
    near, far = pltpu.VMEM, pltpu.HBM
    b_cells = shape((128, cells), BF, far)
    f_square = shape((128, 128), F32, far)
    a_map, b_map = pltpu.VMEM((512, 1024), BF), pltpu.VMEM((1024, 1024), BF)

    send, zn = call(
        operands_kernel, grid,
        [natural, scalar, vec, vec, wide, wide],
        [direct, chan_major],
        [shape((64, 2, 64, 128), BF, near), b_cells],
        [swap] * 2,
    )(pair, length, gain_in, bias_in, w_left, w_right)
    zn = keep(zn, far)
    operands = keep(exchange(send), near)

    *factors, hat_grad, zn_cells = call(
        factors_kernel, grid,
        [chan_major, scalar, natural, vec, wide, wide, square, square],
        [chan_major] * 4 + [single, cell_major],
        [b_cells] * 4 + [shape((64, 64, 128), F32, far), shape((cells, 128), BF, far)],
        [swap],
    )(zn, length, cotangent, gain_p, w_left, w_right, w_gate, w_out)
    factors = [keep(f, far) for f in factors]

    product = call(
        product_kernel, (1,),
        [direct],
        pl.BlockSpec(memory_space=pltpu.HBM),
        shape((8, 8, 64, 128), BF, far),
        [a_map, b_map, pltpu.VMEM((8, 8, 64, 128), BF), pltpu.SemaphoreType.DMA((4,))],
    )(operands).reshape(64, 64, 128)

    product = keep(exchange(product), near)
    send = call(
        middle_kernel, grid,
        [direct, single],
        direct,
        shape((64, 64, 128), BF, near),
    )(product, keep(hat_grad, far))
    got = exchange(send)

    updated, d_gpre, grad_out, grad_gate = call(
        updated_kernel, grid,
        [single, chan_major, natural, vec, vec, square, square],
        [natural, chan_major, square, square],
        [shape(pair.shape, BF, far), b_cells, f_square, f_square],
        [swap],
    )(product, zn, cotangent, gain_p, bias_p, w_out, w_gate)

    send = call(
        product_grads_kernel, (1,),
        [direct, direct],
        whole(64, 2, 64, 128),
        shape((64, 2, 64, 128), BF, far),
        [a_map, b_map, a_map],
    )(keep(got, near), operands)

    grads = keep(exchange(send), near)
    terms = call(
        weights_kernel, grid,
        [direct, cell_major] + [chan_major] * 4 + [square, square],
        whole(64, 16, 128),
        shape((64, 16, 128), BF, far),
        [pltpu.VMEM((512, 128), F32), pltpu.VMEM((1024, 128), F32), swap],
    )(grads, keep(zn_cells, far), *factors, keep(grad_gate, far), keep(grad_out, far))
    shares = exchange(terms)

    d_pair = call(
        pair_kernel, grid,
        [natural, vec, direct] + [chan_major] * 5 + [wide, wide, square],
        natural,
        shape(pair.shape, BF, far),
        [swap],
    )(pair, gain_in, grads, *factors, keep(d_gpre, far), w_left, w_right, w_gate)

    summed = call(
        functools.partial(sum_kernel, 1.0 / total), (1,),
        [whole(64, 16, 128)], whole(64, 16, 128), shape((64, 16, 128), BF, far), cost=(10**6, 10**6),
    )(shares)
    sums = call(
        split_kernel, (1,),
        [whole(64, 16, 128)],
        [wide, wide, square, square],
        [shape((128, 256), F32)] * 2 + [shape((128, 128), F32)] * 2,
        [pltpu.VMEM((1024, 128), F32)],
        cost=(10**6, 10**6),
    )(exchange(summed))
    return (updated, d_pair, *sums)


def solution(mesh):
    in_specs = (
        P(("rep", "row"), "col", None),
        P("rep"),
        P(),
        P(),
        P(),
        P(),
        P(),
        P(),
        P(),
        P(),
        P(("rep", "row"), "col", None),
    )
    out_specs = (
        P(("rep", "row"), "col", None),
        P(("rep", "row"), "col", None),
        P("rep", None),
        P("rep", None),
        P("rep", None),
        P("rep", None),
    )
    return jax.shard_map(body, mesh=mesh, in_specs=in_specs, out_specs=out_specs, check_vma=False)
```

```python
import functools

import jax
import jax.numpy as jnp
from jax import lax
from jax.experimental import pallas as pl
from jax.experimental.pallas import tpu as pltpu
from jax.sharding import PartitionSpec as P

AXES = ("row", "col")
BF = jnp.bfloat16
F32 = jnp.float32
STEP = 32
ROWS = 16
PITCH = 33
PITCH_16 = 17
CELLS = STEP * 64
LIMIT = 32 * 1024 * 1024
EPS = 1e-05


def dot(lhs, rhs, left_dim, right_dim):
    return lax.dot_general(
        lhs, rhs, (((left_dim,), (right_dim,)), ((), ())), preferred_element_type=F32
    )


def column(ref):
    return jnp.transpose(jnp.broadcast_to(ref[...], (128, 128)))[:, :1]


def normalize(values):
    centered = values - jnp.mean(values, axis=0, keepdims=True)
    inverse = lax.rsqrt(jnp.mean(centered * centered, axis=0, keepdims=True) + EPS)
    return centered * inverse, inverse


def normalize_backward(grad_hat, normed, inverse):
    return inverse * (
        grad_hat
        - jnp.mean(grad_hat, axis=0, keepdims=True)
        - normed * jnp.mean(grad_hat * normed, axis=0, keepdims=True)
    )


def sigmoid(values):
    return 0.5 * jnp.tanh(0.5 * values) + 0.5


def spans(rows):
    return [(i, slice(i * 64, (i + rows) * 64)) for i in range(0, STEP, rows)]


def load_transposed(ref, first, rows):
    return jnp.transpose(ref[first : first + rows].reshape(rows * 64, 128)).astype(F32)


def store_transposed(ref, first, values):
    rows = values.shape[1] // 64
    ref[first : first + rows] = jnp.transpose(values.astype(BF)).reshape(rows, 64, 128)


def low_half(dims):
    return lax.broadcasted_iota(jnp.int32, dims, len(dims) - 1) < 64


def pack(values, first, scr):
    low = low_half((64, 128))
    for t in range(values.shape[1] // 128):
        lane = slice(t * 128, (t + 1) * 128)
        upper, lower = values[:64, lane], values[64:, lane]
        row = first + 2 * t
        scr[pl.ds(row, 64, stride=PITCH), :] = jnp.where(low, upper, pltpu.roll(lower, 64, 1))
        scr[pl.ds(row + 1, 64, stride=PITCH), :] = jnp.where(low, pltpu.roll(upper, 64, 1), lower)


def packed(scr, kind=BF):
    return jnp.stack([scr[d * PITCH : d * PITCH + STEP] for d in range(64)]).astype(kind)


def spread(payload, scr):
    wide = payload.astype(F32)
    for d in range(64):
        scr[d * PITCH : d * PITCH + STEP] = wide[d]


def unpack(scr, first, rows):
    low = low_half((64, 128))
    tiles = []
    for row in range(first, first + rows, 2):
        even = scr[pl.ds(row, 64, stride=PITCH), :]
        odd = scr[pl.ds(row + 1, 64, stride=PITCH), :]
        upper = jnp.where(low, even, pltpu.roll(odd, 64, 1))
        lower = jnp.where(low, pltpu.roll(even, 64, 1), odd)
        tiles.append(jnp.concatenate([upper, lower], axis=0))
    return jnp.concatenate(tiles, axis=1) if len(tiles) > 1 else tiles[0]


def cell_mask(length_ref, first, rows):
    cells = lax.broadcasted_iota(jnp.int32, (1, rows * 64), 1)
    row = lax.axis_index("row") * 64 + pl.program_id(0) * STEP + first + cells // 64
    col = lax.axis_index("col") * 64 + cells % 64
    length = length_ref[0]
    return ((row < length) & (col < length)).astype(F32)


def operands_kernel(pair, length, gain_ref, bias_ref, w_left, w_right, send, zn_out, scr_a, scr_b):
    gain, bias = column(gain_ref), column(bias_ref)
    weights = [jnp.transpose(ref[...]) for ref in (w_left, w_right)]
    for first, here in spans(ROWS):
        zhat, _ = normalize(load_transposed(pair, first, ROWS))
        zn = (zhat * gain + bias).astype(BF)
        zn_out[:, here] = zn
        mask = cell_mask(length, first, ROWS)
        for weight, scr in zip(weights, (scr_a, scr_b)):
            both = dot(weight, zn, 1, 0)
            pack(mask * sigmoid(both[128:]) * both[:128], first, scr)
    rows = pl.ds(pl.multiple_of(pl.program_id(0) * STEP, STEP), STEP)
    send[:, 0, rows] = packed(scr_a)
    send[:, 1, rows] = packed(scr_b)


def factors_kernel(
    zn_ref, length, cot, gain_ref, w_left, w_right, w_gate, w_out,
    factors, hat_grad, zn_cells, scr,
):
    gain = column(gain_ref)
    for first, here in spans(ROWS):
        zn = zn_ref[:, here]
        zn_cells[here] = jnp.transpose(zn)
        mask = cell_mask(length, first, ROWS)
        gate = sigmoid(dot(w_gate[...], zn, 0, 0))
        d_proj = (load_transposed(cot, first, ROWS) * gate).astype(BF)
        pack(dot(w_out[...], d_proj, 1, 0) * gain, first, scr)
        for which, weights in enumerate((w_left, w_right)):
            value = dot(weights[...], zn, 0, 0)
            sigma = sigmoid(value[128:])
            factors[which * 256 : which * 256 + 128, here] = (mask * sigma).astype(BF)
            factors[which * 256 + 128 : which * 256 + 256, here] = (mask * value[:128] * sigma * (1.0 - sigma)).astype(BF)
    hat_grad[...] = packed(scr, F32)


def gather_map(got, which, scr):
    for r in range(8):
        for c in range(8):
            scr[r * 64 : (r + 1) * 64, c * 128 : (c + 1) * 128] = got[r * 8 + c, which]


def double_rows(got, which, scr):
    low = low_half((64, 128))
    zero = jnp.zeros((64, 128), BF)
    for r in range(8):
        for c in range(8):
            tile = got[r * 8 + c, which]
            lanes = slice(c * 128, (c + 1) * 128)
            scr[r * 128 : r * 128 + 64, lanes] = jnp.where(low, tile, zero)
            scr[r * 128 + 64 : (r + 1) * 128, lanes] = jnp.where(low, zero, tile)


def product_kernel(got, send, a_scr, b_scr, out_scr, sems):
    gather_map(got, 0, a_scr)
    double_rows(got, 1, b_scr)
    copies = []
    for n in range(4):
        out = dot(a_scr[...], b_scr[n * 256 : (n + 1) * 256, :], 1, 1).astype(BF)
        for r in range(8):
            for c in range(2):
                out_scr[r, 2 * n + c] = out[r * 64 : (r + 1) * 64, c * 128 : (c + 1) * 128]
        part = (slice(None), pl.ds(2 * n, 2))
        copies.append(pltpu.make_async_copy(out_scr.at[part], send.at[part], sems.at[n]))
        copies[-1].start()
    for copy in copies:
        copy.wait()


def halves_sum(values):
    return values + pltpu.roll(values, 64, 1)


def middle_kernel(got, hat_grad, send):
    rows = pl.ds(pl.multiple_of(pl.program_id(0) * STEP, STEP), STEP)

    def value(d):
        return got[d, rows].astype(F32)

    def channel_mean(term):
        sums = [term(d) for d in range(4)]
        for d in range(4, 64):
            sums[d % 4] = sums[d % 4] + term(d)
        return halves_sum((sums[0] + sums[1]) + (sums[2] + sums[3])) * (1.0 / 128)

    mean = channel_mean(value)
    inverse = lax.rsqrt(channel_mean(lambda d: (value(d) - mean) * (value(d) - mean)) + EPS)
    first = channel_mean(lambda d: hat_grad[d])
    second = channel_mean(lambda d: hat_grad[d] * ((value(d) - mean) * inverse))
    for d in range(64):
        hat = (value(d) - mean) * inverse
        send[d, rows] = (inverse * (hat_grad[d] - first - hat * second)).astype(BF)


def updated_kernel(
    product, zn_ref, cot, gain_ref, bias_ref, w_out, w_gate,
    updated, dg_out, grad_out, grad_gate, scr,
):
    @pl.when(pl.program_id(0) == 0)
    def _():
        grad_out[...] = jnp.zeros((128, 128), F32)
        grad_gate[...] = jnp.zeros((128, 128), F32)

    spread(product[...], scr)
    gain, bias = column(gain_ref), column(bias_ref)
    for first, here in spans(ROWS):
        hat, _ = normalize(unpack(scr, first, ROWS))
        y = (hat * gain + bias).astype(BF)
        zn = zn_ref[:, here]
        gate = sigmoid(dot(w_gate[...], zn, 0, 0))
        upstream = load_transposed(cot, first, ROWS)
        proj = dot(w_out[...], y, 0, 0)
        d_proj = (upstream * gate).astype(BF)
        d_gpre = (upstream * proj * gate * (1.0 - gate)).astype(BF)
        store_transposed(updated, first, gate * proj)
        dg_out[:, here] = d_gpre
        grad_out[...] += dot(y, d_proj, 1, 1)
        grad_gate[...] += dot(zn, d_gpre, 1, 1)


def product_grads_kernel(got, operands_ref, send, a_scr, b_scr, d_scr, out_scr, sems):
    def copy(which):
        part = (slice(None), which)
        return pltpu.make_async_copy(out_scr.at[part], send.at[part], sems.at[which])

    gather_map(operands_ref, 0, a_scr)
    double_rows(operands_ref, 1, b_scr)
    for r in range(8):
        for c in range(8):
            d_scr[r * 64 : (r + 1) * 64, c * 128 : (c + 1) * 128] = got[r * 8 + c]
    for n in range(4):
        out = dot(d_scr[...], b_scr[:, n * 256 : (n + 1) * 256], 1, 0).astype(BF)
        for r in range(8):
            for c in range(2):
                out_scr[r * 8 + 2 * n + c, 0] = out[r * 64 : (r + 1) * 64, c * 128 : (c + 1) * 128]
    copy(0).start()
    low = low_half((64, 128))
    for m in range(2):
        out = dot(d_scr[:, m * 512 : (m + 1) * 512], a_scr[...], 0, 0)
        for r in range(4):
            for c in range(8):
                lanes = slice(c * 128, (c + 1) * 128)
                out_scr[(m * 4 + r) * 8 + c, 1] = jnp.where(
                    low, out[r * 128 : r * 128 + 64, lanes], out[r * 128 + 64 : (r + 1) * 128, lanes]
                ).astype(BF)
    copy(1).start()
    copy(0).wait()
    copy(1).wait()


def cell_grads(got, which, factors, scr):
    rows = pl.ds(pl.multiple_of(pl.program_id(0) * STEP, STEP), STEP)
    spread(got[:, which, rows], scr)
    grad = unpack(scr, 0, STEP)
    slope = factors[which * 256 : which * 256 + 128]
    bend = factors[which * 256 + 128 : which * 256 + 256]
    return jnp.concatenate([grad * slope, grad * bend], axis=0).astype(BF)


def weights_kernel(
    got, zn_cells, factors, grad_gate, grad_out, send, acc, stage, scr
):
    @pl.when(pl.program_id(0) == 0)
    def _():
        acc[...] = jnp.zeros((512, 128), F32)

    for which in range(2):
        grads = cell_grads(got, which, factors, scr)
        acc[which * 256 : (which + 1) * 256] += dot(grads, zn_cells[...], 1, 0)

    @pl.when(pl.program_id(0) == pl.num_programs(0) - 1)
    def _():
        for t in range(6):
            if t < 4:
                tile = acc[t * 128 : (t + 1) * 128]
            else:
                tile = (grad_gate if t == 4 else grad_out)[...]
            for half in range(2):
                stage[pl.ds(2 * t + half, 64, stride=PITCH_16), :] = tile[half * 64 : (half + 1) * 64]
        for t in range(12, 16):
            stage[pl.ds(t, 64, stride=PITCH_16), :] = jnp.zeros((64, 128), F32)
        send[...] = jnp.stack([stage[d * PITCH_16 : d * PITCH_16 + 16] for d in range(64)]).astype(BF)


def pair_kernel(pair, gain_ref, got, factors, dg, w_left, w_right, w_gate, out, scr):
    gain = column(gain_ref)
    d_left = cell_grads(got, 0, factors, scr)
    d_right = cell_grads(got, 1, factors, scr)
    for first, here in spans(ROWS):
        zhat, inverse = normalize(load_transposed(pair, first, ROWS))
        d_zn = (
            dot(w_left[...], d_left[:, here], 1, 0)
            + dot(w_right[...], d_right[:, here], 1, 0)
            + dot(w_gate[...], dg[:, here], 1, 0)
        )
        store_transposed(out, first, normalize_backward(d_zn * gain, zhat, inverse))


def sum_kernel(scale, got, send):
    total = got[0].astype(F32)
    for s in range(1, 64):
        total = total + got[s].astype(F32)
    send[...] = jnp.broadcast_to((total * scale).astype(BF)[None], send.shape)


def split_kernel(got, left, right, gate, out, stage):
    wide = got[...].astype(F32)
    for d in range(64):
        stage[d * PITCH_16 : d * PITCH_16 + 16] = wide[d]
    for t, (ref, lane) in enumerate(
        ((left, 0), (left, 128), (right, 0), (right, 128), (gate, 0), (out, 0))
    ):
        tile = jnp.concatenate(
            [stage[pl.ds(2 * t + half, 64, stride=PITCH_16), :] for half in range(2)], axis=0
        )
        ref[:, lane : lane + 128] = jnp.transpose(tile) if t < 4 else tile


def call(kernel, grid, in_specs, out_specs, out_shape, scratch=(), cost=(10**9, 10**7)):
    return pl.pallas_call(
        kernel,
        grid=grid,
        in_specs=in_specs,
        out_specs=out_specs,
        out_shape=out_shape,
        scratch_shapes=list(scratch),
        cost_estimate=pl.CostEstimate(flops=cost[0], bytes_accessed=cost[1], transcendentals=0),
        compiler_params=pltpu.CompilerParams(vmem_limit_bytes=LIMIT),
    )


def whole(*dims):
    return pl.BlockSpec(dims, lambda *_: (0,) * len(dims))


def shape(dims, kind, space=None):
    return jax.ShapeDtypeStruct(dims, kind) if space is None else space(dims, kind)


def keep(value, space):
    return pltpu.with_memory_space_constraint(value, space)


def exchange(values):
    owners = values.shape[0]
    flat = values.reshape(owners, -1, 128)
    return lax.all_to_all(flat, AXES, 0, 0, tiled=True).reshape(values.shape)


def body(
    pair, length, ln_in_gain, ln_in_bias, w_left, w_right, w_gate,
    product_norm_gain, product_norm_bias, w_out, cotangent,
):
    tile_i, tile_j, chans = pair.shape
    total = tile_j * lax.axis_size("col")
    cells = tile_i * tile_j
    grid = (tile_i // STEP,)
    gain_in, bias_in = ln_in_gain.reshape(1, 128), ln_in_bias.reshape(1, 128)
    gain_p, bias_p = product_norm_gain.reshape(1, 128), product_norm_bias.reshape(1, 128)
    pair, cotangent = keep(pair, pltpu.HBM), keep(cotangent, pltpu.HBM)
    w_left, w_right, w_gate, w_out = (
        keep(w, pltpu.HBM) for w in (w_left, w_right, w_gate, w_out)
    )

    natural = pl.BlockSpec((STEP, 64, 128), lambda i: (i, 0, 0))
    chan_major = pl.BlockSpec((128, CELLS), lambda i: (0, i))
    chan_major4 = pl.BlockSpec((512, CELLS), lambda i: (0, i))
    cell_major = pl.BlockSpec((CELLS, 128), lambda i: (i, 0))
    single = pl.BlockSpec((64, STEP, 128), lambda i: (0, i, 0))
    double = pl.BlockSpec((64, 2, STEP, 128), lambda i: (0, 0, i, 0))
    direct = pl.BlockSpec(memory_space=pltpu.VMEM)
    scalar = pl.BlockSpec(memory_space=pltpu.SMEM)
    vec, wide, square = whole(1, 128), whole(128, 256), whole(128, 128)
    swap = pltpu.VMEM((64 * PITCH, 128), F32)
    near, far = pltpu.VMEM, pltpu.HBM
    b_cells = shape((128, cells), BF, far)
    f_square = shape((128, 128), F32, far)
    a_map, b_map = pltpu.VMEM((512, 1024), BF), pltpu.VMEM((1024, 1024), BF)

    send, zn = call(
        operands_kernel, grid,
        [natural, scalar, vec, vec, wide, wide],
        [direct, chan_major],
        [shape((64, 2, 64, 128), BF, near), b_cells],
        [swap] * 2,
    )(pair, length, gain_in, bias_in, w_left, w_right)
    zn = keep(zn, far)
    operands = keep(exchange(send), near)

    factors, hat_grad, zn_cells = call(
        factors_kernel, grid,
        [chan_major, scalar, natural, vec, wide, wide, square, square],
        [chan_major4, single, cell_major],
        [shape((512, cells), BF, far), shape((64, 64, 128), F32, far), shape((cells, 128), BF, far)],
        [swap],
    )(zn, length, cotangent, gain_p, w_left, w_right, w_gate, w_out)
    factors = keep(factors, far)

    product = call(
        product_kernel, (1,),
        [direct],
        pl.BlockSpec(memory_space=pltpu.HBM),
        shape((8, 8, 64, 128), BF, far),
        [a_map, b_map, pltpu.VMEM((8, 8, 64, 128), BF), pltpu.SemaphoreType.DMA((4,))],
    )(operands).reshape(64, 64, 128)

    product = keep(exchange(product), near)
    send = call(
        middle_kernel, grid,
        [direct, single],
        direct,
        shape((64, 64, 128), BF, near),
    )(product, keep(hat_grad, far))
    got = exchange(send)

    updated, d_gpre, grad_out, grad_gate = call(
        updated_kernel, grid,
        [single, chan_major, natural, vec, vec, square, square],
        [natural, chan_major, square, square],
        [shape(pair.shape, BF, far), b_cells, f_square, f_square],
        [swap],
    )(product, zn, cotangent, gain_p, bias_p, w_out, w_gate)

    send = call(
        product_grads_kernel, (1,),
        [direct, direct],
        pl.BlockSpec(memory_space=pltpu.HBM),
        shape((64, 2, 64, 128), BF, far),
        [a_map, b_map, a_map, pltpu.VMEM((64, 2, 64, 128), BF), pltpu.SemaphoreType.DMA((2,))],
    )(keep(got, near), operands)

    grads = keep(exchange(send), near)
    terms = call(
        weights_kernel, grid,
        [direct, cell_major, chan_major4] + [square, square],
        whole(64, 16, 128),
        shape((64, 16, 128), BF, far),
        [pltpu.VMEM((512, 128), F32), pltpu.VMEM((64 * PITCH_16, 128), F32), swap],
    )(grads, keep(zn_cells, far), factors, keep(grad_gate, far), keep(grad_out, far))
    shares = exchange(terms)

    d_pair = call(
        pair_kernel, grid,
        [natural, vec, direct, chan_major4, chan_major] + [wide, wide, square],
        natural,
        shape(pair.shape, BF, far),
        [swap],
    )(pair, gain_in, grads, factors, keep(d_gpre, far), w_left, w_right, w_gate)

    summed = call(
        functools.partial(sum_kernel, 1.0 / total), (1,),
        [direct], whole(64, 16, 128), shape((64, 16, 128), BF, far), cost=(10**6, 10**6),
    )(keep(shares, near))
    sums = call(
        split_kernel, (1,),
        [whole(64, 16, 128)],
        [wide, wide, square, square],
        [shape((128, 256), F32)] * 2 + [shape((128, 128), F32)] * 2,
        [pltpu.VMEM((64 * PITCH_16, 128), F32)],
        cost=(10**6, 10**6),
    )(exchange(summed))
    return (updated, d_pair, *sums)


def solution(mesh):
    in_specs = (
        P(("rep", "row"), "col", None),
        P("rep"),
        P(),
        P(),
        P(),
        P(),
        P(),
        P(),
        P(),
        P(),
        P(("rep", "row"), "col", None),
    )
    out_specs = (
        P(("rep", "row"), "col", None),
        P(("rep", "row"), "col", None),
        P("rep", None),
        P("rep", None),
        P("rep", None),
        P("rep", None),
    )
    return jax.shard_map(body, mesh=mesh, in_specs=in_specs, out_specs=out_specs, check_vma=False)
```

```python
import functools

import jax
import jax.numpy as jnp
from jax import lax
from jax.experimental import pallas as pl
from jax.experimental.pallas import tpu as pltpu
from jax.sharding import PartitionSpec as P

AXES = ("row", "col")
BF = jnp.bfloat16
F32 = jnp.float32
STEP = 32
ROWS = 16
PITCH = 33
PITCH_16 = 17
CELLS = STEP * 64
LIMIT = 32 * 1024 * 1024
EPS = 1e-05


def dot(lhs, rhs, left_dim, right_dim):
    return lax.dot_general(
        lhs, rhs, (((left_dim,), (right_dim,)), ((), ())), preferred_element_type=F32
    )


def column(ref):
    return jnp.transpose(jnp.broadcast_to(ref[...], (128, 128)))[:, :1]


def normalize(values):
    centered = values - jnp.mean(values, axis=0, keepdims=True)
    inverse = lax.rsqrt(jnp.mean(centered * centered, axis=0, keepdims=True) + EPS)
    return centered * inverse, inverse


def normalize_backward(grad_hat, normed, inverse):
    return inverse * (
        grad_hat
        - jnp.mean(grad_hat, axis=0, keepdims=True)
        - normed * jnp.mean(grad_hat * normed, axis=0, keepdims=True)
    )


def sigmoid(values):
    return 0.5 * jnp.tanh(0.5 * values) + 0.5


def spans(rows):
    return [(i, slice(i * 64, (i + rows) * 64)) for i in range(0, STEP, rows)]


def load_transposed(ref, first, rows):
    return jnp.transpose(ref[first : first + rows].reshape(rows * 64, 128)).astype(F32)


def store_transposed(ref, first, values):
    rows = values.shape[1] // 64
    ref[first : first + rows] = jnp.transpose(values.astype(BF)).reshape(rows, 64, 128)


def low_half(dims):
    return lax.broadcasted_iota(jnp.int32, dims, len(dims) - 1) < 64


def pack(values, first, scr):
    low = low_half((64, 128))
    for t in range(values.shape[1] // 128):
        lane = slice(t * 128, (t + 1) * 128)
        upper, lower = values[:64, lane], values[64:, lane]
        row = first + 2 * t
        scr[pl.ds(row, 64, stride=PITCH), :] = jnp.where(low, upper, pltpu.roll(lower, 64, 1))
        scr[pl.ds(row + 1, 64, stride=PITCH), :] = jnp.where(low, pltpu.roll(upper, 64, 1), lower)


def packed(scr, kind=BF):
    return jnp.stack([scr[d * PITCH : d * PITCH + STEP] for d in range(64)]).astype(kind)


def spread(payload, scr):
    wide = payload.astype(F32)
    for d in range(64):
        scr[d * PITCH : d * PITCH + STEP] = wide[d]


def unpack(scr, first, rows):
    low = low_half((64, 128))
    tiles = []
    for row in range(first, first + rows, 2):
        even = scr[pl.ds(row, 64, stride=PITCH), :]
        odd = scr[pl.ds(row + 1, 64, stride=PITCH), :]
        upper = jnp.where(low, even, pltpu.roll(odd, 64, 1))
        lower = jnp.where(low, pltpu.roll(even, 64, 1), odd)
        tiles.append(jnp.concatenate([upper, lower], axis=0))
    return jnp.concatenate(tiles, axis=1) if len(tiles) > 1 else tiles[0]


def cell_mask(length_ref, first, rows):
    cells = lax.broadcasted_iota(jnp.int32, (1, rows * 64), 1)
    row = lax.axis_index("row") * 64 + pl.program_id(0) * STEP + first + cells // 64
    col = lax.axis_index("col") * 64 + cells % 64
    length = length_ref[0]
    return ((row < length) & (col < length)).astype(F32)


def operands_kernel(pair, length, gain_ref, bias_ref, w_left, w_right, send, zn_out, scr_a, scr_b):
    gain, bias = column(gain_ref), column(bias_ref)
    weights = [jnp.transpose(ref[...]) for ref in (w_left, w_right)]
    for first, here in spans(ROWS):
        zhat, _ = normalize(load_transposed(pair, first, ROWS))
        zn = (zhat * gain + bias).astype(BF)
        zn_out[:, here] = zn
        mask = cell_mask(length, first, ROWS)
        for weight, scr in zip(weights, (scr_a, scr_b)):
            both = dot(weight, zn, 1, 0)
            pack(mask * sigmoid(both[128:]) * both[:128], first, scr)
    rows = pl.ds(pl.multiple_of(pl.program_id(0) * STEP, STEP), STEP)
    send[:, 0, rows] = packed(scr_a)
    send[:, 1, rows] = packed(scr_b)


def factors_kernel(
    zn_ref, length, cot, gain_ref, w_left, w_right, w_gate, w_out,
    factors, hat_grad, zn_cells, scr,
):
    gain = column(gain_ref)
    for first, here in spans(ROWS):
        zn = zn_ref[:, here]
        zn_cells[here] = jnp.transpose(zn)
        mask = cell_mask(length, first, ROWS)
        gate = sigmoid(dot(w_gate[...], zn, 0, 0))
        d_proj = (load_transposed(cot, first, ROWS) * gate).astype(BF)
        pack(dot(w_out[...], d_proj, 1, 0) * gain, first, scr)
        for which, weights in enumerate((w_left, w_right)):
            value = dot(weights[...], zn, 0, 0)
            sigma = sigmoid(value[128:])
            factors[which * 256 : which * 256 + 128, here] = (mask * sigma).astype(BF)
            factors[which * 256 + 128 : which * 256 + 256, here] = (mask * value[:128] * sigma * (1.0 - sigma)).astype(BF)
    hat_grad[...] = packed(scr, F32)


def gather_map(got, which, scr):
    for r in range(8):
        for c in range(8):
            scr[r * 64 : (r + 1) * 64, c * 128 : (c + 1) * 128] = got[r * 8 + c, which]


def double_rows(got, which, scr):
    low = low_half((64, 128))
    zero = jnp.zeros((64, 128), BF)
    for r in range(8):
        for c in range(8):
            tile = got[r * 8 + c, which]
            lanes = slice(c * 128, (c + 1) * 128)
            scr[r * 128 : r * 128 + 64, lanes] = jnp.where(low, tile, zero)
            scr[r * 128 + 64 : (r + 1) * 128, lanes] = jnp.where(low, zero, tile)


def product_kernel(got, send, a_scr, b_scr, out_scr, sems):
    gather_map(got, 0, a_scr)
    double_rows(got, 1, b_scr)
    copies = []
    for n in range(4):
        out = dot(a_scr[...], b_scr[n * 256 : (n + 1) * 256, :], 1, 1).astype(BF)
        for r in range(8):
            for c in range(2):
                out_scr[r, 2 * n + c] = out[r * 64 : (r + 1) * 64, c * 128 : (c + 1) * 128]
        part = (slice(None), pl.ds(2 * n, 2))
        copies.append(pltpu.make_async_copy(out_scr.at[part], send.at[part], sems.at[n]))
        copies[-1].start()
    for copy in copies:
        copy.wait()


def halves_sum(values):
    return values + pltpu.roll(values, 64, 1)


def middle_kernel(got, hat_grad, send):
    rows = pl.ds(pl.multiple_of(pl.program_id(0) * STEP, STEP), STEP)

    def value(d):
        return got[d, rows].astype(F32)

    def channel_mean(term):
        sums = [term(d) for d in range(4)]
        for d in range(4, 64):
            sums[d % 4] = sums[d % 4] + term(d)
        return halves_sum((sums[0] + sums[1]) + (sums[2] + sums[3])) * (1.0 / 128)

    mean = channel_mean(value)
    inverse = lax.rsqrt(channel_mean(lambda d: (value(d) - mean) * (value(d) - mean)) + EPS)
    first = channel_mean(lambda d: hat_grad[d])
    second = channel_mean(lambda d: hat_grad[d] * ((value(d) - mean) * inverse))
    for d in range(64):
        hat = (value(d) - mean) * inverse
        send[d, rows] = (inverse * (hat_grad[d] - first - hat * second)).astype(BF)


def updated_kernel(
    product, zn_ref, cot, gain_ref, bias_ref, w_out, w_gate,
    updated, dg_out, grad_out, grad_gate, scr,
):
    @pl.when(pl.program_id(0) == 0)
    def _():
        grad_out[...] = jnp.zeros((128, 128), F32)
        grad_gate[...] = jnp.zeros((128, 128), F32)

    spread(product[...], scr)
    gain, bias = column(gain_ref), column(bias_ref)
    for first, here in spans(ROWS):
        hat, _ = normalize(unpack(scr, first, ROWS))
        y = (hat * gain + bias).astype(BF)
        zn = zn_ref[:, here]
        gate = sigmoid(dot(w_gate[...], zn, 0, 0))
        upstream = load_transposed(cot, first, ROWS)
        proj = dot(w_out[...], y, 0, 0)
        d_proj = (upstream * gate).astype(BF)
        d_gpre = (upstream * proj * gate * (1.0 - gate)).astype(BF)
        store_transposed(updated, first, gate * proj)
        dg_out[:, here] = d_gpre
        grad_out[...] += dot(y, d_proj, 1, 1)
        grad_gate[...] += dot(zn, d_gpre, 1, 1)


def product_grads_kernel(got, operands_ref, send, a_scr, b_scr, d_scr, out_scr, sems):
    def copy(which):
        part = (slice(None), which)
        return pltpu.make_async_copy(out_scr.at[part], send.at[part], sems.at[which])

    gather_map(operands_ref, 0, a_scr)
    double_rows(operands_ref, 1, b_scr)
    for r in range(8):
        for c in range(8):
            d_scr[r * 64 : (r + 1) * 64, c * 128 : (c + 1) * 128] = got[r * 8 + c]
    for n in range(4):
        out = dot(d_scr[...], b_scr[:, n * 256 : (n + 1) * 256], 1, 0).astype(BF)
        for r in range(8):
            for c in range(2):
                out_scr[r * 8 + 2 * n + c, 0] = out[r * 64 : (r + 1) * 64, c * 128 : (c + 1) * 128]
    copy(0).start()
    low = low_half((64, 128))
    for m in range(2):
        out = dot(d_scr[:, m * 512 : (m + 1) * 512], a_scr[...], 0, 0)
        for r in range(4):
            for c in range(8):
                lanes = slice(c * 128, (c + 1) * 128)
                out_scr[(m * 4 + r) * 8 + c, 1] = jnp.where(
                    low, out[r * 128 : r * 128 + 64, lanes], out[r * 128 + 64 : (r + 1) * 128, lanes]
                ).astype(BF)
    copy(1).start()
    copy(0).wait()
    copy(1).wait()


def cell_grads(got, which, factors, scr):
    rows = pl.ds(pl.multiple_of(pl.program_id(0) * STEP, STEP), STEP)
    spread(got[:, which, rows], scr)
    grad = unpack(scr, 0, STEP)
    slope = factors[which * 256 : which * 256 + 128]
    bend = factors[which * 256 + 128 : which * 256 + 256]
    return jnp.concatenate([grad * slope, grad * bend], axis=0).astype(BF)


def weights_kernel(
    got, zn_cells, factors, grad_gate, grad_out, send, acc, stage, scr
):
    @pl.when(pl.program_id(0) == 0)
    def _():
        acc[...] = jnp.zeros((512, 128), F32)

    for which in range(2):
        grads = cell_grads(got, which, factors, scr)
        acc[which * 256 : (which + 1) * 256] += dot(grads, zn_cells[...], 1, 0)

    @pl.when(pl.program_id(0) == pl.num_programs(0) - 1)
    def _():
        for t in range(6):
            if t < 4:
                tile = acc[t * 128 : (t + 1) * 128]
            else:
                tile = (grad_gate if t == 4 else grad_out)[...]
            for half in range(2):
                stage[pl.ds(2 * t + half, 64, stride=PITCH_16), :] = tile[half * 64 : (half + 1) * 64]
        for t in range(12, 16):
            stage[pl.ds(t, 64, stride=PITCH_16), :] = jnp.zeros((64, 128), F32)
        send[...] = jnp.stack([stage[d * PITCH_16 : d * PITCH_16 + 16] for d in range(64)]).astype(BF)


def pair_kernel(pair, gain_ref, got, factors, dg, w_left, w_right, w_gate, out, scr):
    gain = column(gain_ref)
    d_left = cell_grads(got, 0, factors, scr)
    d_right = cell_grads(got, 1, factors, scr)
    for first, here in spans(ROWS):
        zhat, inverse = normalize(load_transposed(pair, first, ROWS))
        d_zn = (
            dot(w_left[...], d_left[:, here], 1, 0)
            + dot(w_right[...], d_right[:, here], 1, 0)
            + dot(w_gate[...], dg[:, here], 1, 0)
        )
        store_transposed(out, first, normalize_backward(d_zn * gain, zhat, inverse))


def sum_kernel(scale, got, send):
    total = got[0].astype(F32)
    for s in range(1, 64):
        total = total + got[s].astype(F32)
    send[...] = jnp.broadcast_to((total * scale).astype(BF)[None], send.shape)


def split_kernel(got, left, right, gate, out, stage):
    wide = got[...].astype(F32)
    for d in range(64):
        stage[d * PITCH_16 : d * PITCH_16 + 16] = wide[d]
    for t, (ref, lane) in enumerate(
        ((left, 0), (left, 128), (right, 0), (right, 128), (gate, 0), (out, 0))
    ):
        tile = jnp.concatenate(
            [stage[pl.ds(2 * t + half, 64, stride=PITCH_16), :] for half in range(2)], axis=0
        )
        ref[:, lane : lane + 128] = jnp.transpose(tile) if t < 4 else tile


def call(kernel, grid, in_specs, out_specs, out_shape, scratch=(), cost=(10**9, 10**7)):
    return pl.pallas_call(
        kernel,
        grid=grid,
        in_specs=in_specs,
        out_specs=out_specs,
        out_shape=out_shape,
        scratch_shapes=list(scratch),
        cost_estimate=pl.CostEstimate(flops=cost[0], bytes_accessed=cost[1], transcendentals=0),
        compiler_params=pltpu.CompilerParams(vmem_limit_bytes=LIMIT),
    )


def whole(*dims):
    return pl.BlockSpec(dims, lambda *_: (0,) * len(dims))


def shape(dims, kind, space=None):
    return jax.ShapeDtypeStruct(dims, kind) if space is None else space(dims, kind)


def keep(value, space):
    return pltpu.with_memory_space_constraint(value, space)


def exchange(values):
    owners = values.shape[0]
    flat = values.reshape(owners, -1, 128)
    return lax.all_to_all(flat, AXES, 0, 0, tiled=True).reshape(values.shape)


def body(
    pair, length, ln_in_gain, ln_in_bias, w_left, w_right, w_gate,
    product_norm_gain, product_norm_bias, w_out, cotangent,
):
    tile_i, tile_j, chans = pair.shape
    total = tile_j * lax.axis_size("col")
    cells = tile_i * tile_j
    grid = (tile_i // STEP,)
    gain_in, bias_in = ln_in_gain.reshape(1, 128), ln_in_bias.reshape(1, 128)
    gain_p, bias_p = product_norm_gain.reshape(1, 128), product_norm_bias.reshape(1, 128)
    pair, cotangent = keep(pair, pltpu.HBM), keep(cotangent, pltpu.HBM)
    w_left, w_right, w_gate, w_out = (
        keep(w, pltpu.HBM) for w in (w_left, w_right, w_gate, w_out)
    )

    natural = pl.BlockSpec((STEP, 64, 128), lambda i: (i, 0, 0))
    chan_major = pl.BlockSpec((128, CELLS), lambda i: (0, i))
    chan_major4 = pl.BlockSpec((512, CELLS), lambda i: (0, i))
    cell_major = pl.BlockSpec((CELLS, 128), lambda i: (i, 0))
    single = pl.BlockSpec((64, STEP, 128), lambda i: (0, i, 0))
    double = pl.BlockSpec((64, 2, STEP, 128), lambda i: (0, 0, i, 0))
    direct = pl.BlockSpec(memory_space=pltpu.VMEM)
    scalar = pl.BlockSpec(memory_space=pltpu.SMEM)
    vec, wide, square = whole(1, 128), whole(128, 256), whole(128, 128)
    swap = pltpu.VMEM((66 * PITCH - 2, 128), F32)
    near, far = pltpu.VMEM, pltpu.HBM
    b_cells = shape((128, cells), BF, far)
    f_square = shape((128, 128), F32, far)
    a_map, b_map = pltpu.VMEM((512, 1024), BF), pltpu.VMEM((1024, 1024), BF)

    send, zn = call(
        operands_kernel, grid,
        [natural, scalar, vec, vec, wide, wide],
        [direct, chan_major],
        [shape((64, 2, 64, 128), BF, near), b_cells],
        [swap] * 2,
    )(pair, length, gain_in, bias_in, w_left, w_right)
    zn = keep(zn, far)
    operands = keep(exchange(send), near)

    factors, hat_grad, zn_cells = call(
        factors_kernel, grid,
        [chan_major, scalar, natural, vec, wide, wide, square, square],
        [chan_major4, single, cell_major],
        [shape((512, cells), BF, far), shape((64, 64, 128), F32, far), shape((cells, 128), BF, far)],
        [swap],
    )(zn, length, cotangent, gain_p, w_left, w_right, w_gate, w_out)
    factors = keep(factors, far)

    product = call(
        product_kernel, (1,),
        [direct],
        pl.BlockSpec(memory_space=pltpu.HBM),
        shape((8, 8, 64, 128), BF, far),
        [a_map, b_map, pltpu.VMEM((8, 8, 64, 128), BF), pltpu.SemaphoreType.DMA((4,))],
    )(operands).reshape(64, 64, 128)

    product = keep(exchange(product), near)
    send = call(
        middle_kernel, grid,
        [direct, single],
        direct,
        shape((64, 64, 128), BF, near),
    )(product, keep(hat_grad, far))
    got = exchange(send)

    updated, d_gpre, grad_out, grad_gate = call(
        updated_kernel, grid,
        [single, chan_major, natural, vec, vec, square, square],
        [natural, chan_major, square, square],
        [shape(pair.shape, BF, far), b_cells, f_square, f_square],
        [swap],
    )(product, zn, cotangent, gain_p, bias_p, w_out, w_gate)

    send = call(
        product_grads_kernel, (1,),
        [direct, direct],
        pl.BlockSpec(memory_space=pltpu.HBM),
        shape((64, 2, 64, 128), BF, far),
        [a_map, b_map, a_map, pltpu.VMEM((64, 2, 64, 128), BF), pltpu.SemaphoreType.DMA((2,))],
    )(keep(got, near), operands)

    grads = keep(exchange(send), near)
    terms = call(
        weights_kernel, grid,
        [direct, cell_major, chan_major4] + [square, square],
        whole(64, 16, 128),
        shape((64, 16, 128), BF, far),
        [pltpu.VMEM((512, 128), F32), pltpu.VMEM((66 * PITCH_16 - 2, 128), F32), swap],
    )(grads, keep(zn_cells, far), factors, keep(grad_gate, far), keep(grad_out, far))
    shares = exchange(terms)

    d_pair = call(
        pair_kernel, grid,
        [natural, vec, direct, chan_major4, chan_major] + [wide, wide, square],
        natural,
        shape(pair.shape, BF, far),
        [swap],
    )(pair, gain_in, grads, factors, keep(d_gpre, far), w_left, w_right, w_gate)

    summed = call(
        functools.partial(sum_kernel, 1.0 / total), (1,),
        [direct], whole(64, 16, 128), shape((64, 16, 128), BF, far), cost=(10**6, 10**6),
    )(keep(shares, near))
    sums = call(
        split_kernel, (1,),
        [whole(64, 16, 128)],
        [wide, wide, square, square],
        [shape((128, 256), F32)] * 2 + [shape((128, 128), F32)] * 2,
        [pltpu.VMEM((66 * PITCH_16 - 2, 128), F32)],
        cost=(10**6, 10**6),
    )(exchange(summed))
    return (updated, d_pair, *sums)


def solution(mesh):
    in_specs = (
        P(("rep", "row"), "col", None),
        P("rep"),
        P(),
        P(),
        P(),
        P(),
        P(),
        P(),
        P(),
        P(),
        P(("rep", "row"), "col", None),
    )
    out_specs = (
        P(("rep", "row"), "col", None),
        P(("rep", "row"), "col", None),
        P("rep", None),
        P("rep", None),
        P("rep", None),
        P("rep", None),
    )
    return jax.shard_map(body, mesh=mesh, in_specs=in_specs, out_specs=out_specs, check_vma=False)
```

```python
import functools

import jax
import jax.numpy as jnp
from jax import lax
from jax.experimental import pallas as pl
from jax.experimental.pallas import tpu as pltpu
from jax.sharding import PartitionSpec as P

AXES = ("row", "col")
BF = jnp.bfloat16
F32 = jnp.float32
STEP = 32
ROWS = 16
PITCH = 33
PITCH_16 = 17
CELLS = STEP * 64
LIMIT = 32 * 1024 * 1024
EPS = 1e-05


def dot(lhs, rhs, left_dim, right_dim):
    return lax.dot_general(
        lhs, rhs, (((left_dim,), (right_dim,)), ((), ())), preferred_element_type=F32
    )


def column(ref):
    return jnp.transpose(jnp.broadcast_to(ref[...], (128, 128)))[:, :1]


def normalize(values):
    centered = values - jnp.mean(values, axis=0, keepdims=True)
    inverse = lax.rsqrt(jnp.mean(centered * centered, axis=0, keepdims=True) + EPS)
    return centered * inverse, inverse


def normalize_backward(grad_hat, normed, inverse):
    return inverse * (
        grad_hat
        - jnp.mean(grad_hat, axis=0, keepdims=True)
        - normed * jnp.mean(grad_hat * normed, axis=0, keepdims=True)
    )


def sigmoid(values):
    return 0.5 * jnp.tanh(0.5 * values) + 0.5


def spans(rows):
    return [(i, slice(i * 64, (i + rows) * 64)) for i in range(0, STEP, rows)]


def load_transposed(ref, first, rows):
    return jnp.transpose(ref[first : first + rows].reshape(rows * 64, 128)).astype(F32)


def store_transposed(ref, first, values):
    rows = values.shape[1] // 64
    ref[first : first + rows] = jnp.transpose(values.astype(BF)).reshape(rows, 64, 128)


def low_half(dims):
    return lax.broadcasted_iota(jnp.int32, dims, len(dims) - 1) < 64


def pack(values, first, scr):
    low = low_half((64, 128))
    for t in range(values.shape[1] // 128):
        lane = slice(t * 128, (t + 1) * 128)
        upper, lower = values[:64, lane], values[64:, lane]
        row = first + 2 * t
        scr[pl.ds(row, 64, stride=PITCH), :] = jnp.where(low, upper, pltpu.roll(lower, 64, 1))
        scr[pl.ds(row + 1, 64, stride=PITCH), :] = jnp.where(low, pltpu.roll(upper, 64, 1), lower)


def packed(scr, kind=BF):
    return jnp.stack([scr[d * PITCH : d * PITCH + STEP] for d in range(64)]).astype(kind)


def spread(payload, scr):
    wide = payload.astype(F32)
    for d in range(64):
        scr[d * PITCH : d * PITCH + STEP] = wide[d]


def unpack(scr, first, rows):
    low = low_half((64, 128))
    tiles = []
    for row in range(first, first + rows, 2):
        even = scr[pl.ds(row, 64, stride=PITCH), :]
        odd = scr[pl.ds(row + 1, 64, stride=PITCH), :]
        upper = jnp.where(low, even, pltpu.roll(odd, 64, 1))
        lower = jnp.where(low, pltpu.roll(even, 64, 1), odd)
        tiles.append(jnp.concatenate([upper, lower], axis=0))
    return jnp.concatenate(tiles, axis=1) if len(tiles) > 1 else tiles[0]


def cell_mask(length_ref, first, rows):
    cells = lax.broadcasted_iota(jnp.int32, (1, rows * 64), 1)
    row = lax.axis_index("row") * 64 + pl.program_id(0) * STEP + first + cells // 64
    col = lax.axis_index("col") * 64 + cells % 64
    length = length_ref[0]
    return ((row < length) & (col < length)).astype(F32)


def operands_kernel(pair, length, gain_ref, bias_ref, w_left, w_right, send, zn_out, scr_a, scr_b):
    gain, bias = column(gain_ref), column(bias_ref)
    weights = [jnp.transpose(ref[...]) for ref in (w_left, w_right)]
    for first, here in spans(ROWS):
        zhat, _ = normalize(load_transposed(pair, first, ROWS))
        zn = (zhat * gain + bias).astype(BF)
        zn_out[:, here] = zn
        mask = cell_mask(length, first, ROWS)
        for weight, scr in zip(weights, (scr_a, scr_b)):
            both = dot(weight, zn, 1, 0)
            pack(mask * sigmoid(both[128:]) * both[:128], first, scr)
    rows = pl.ds(pl.multiple_of(pl.program_id(0) * STEP, STEP), STEP)
    send[:, 0, rows] = packed(scr_a)
    send[:, 1, rows] = packed(scr_b)


def factors_kernel(
    zn_ref, length, cot, gain_ref, w_left, w_right, w_gate, w_out,
    factors, hat_grad, zn_cells, scr,
):
    gain = column(gain_ref)
    for first, here in spans(ROWS):
        zn = zn_ref[:, here]
        zn_cells[here] = jnp.transpose(zn)
        mask = cell_mask(length, first, ROWS)
        gate = sigmoid(dot(w_gate[...], zn, 0, 0))
        d_proj = (load_transposed(cot, first, ROWS) * gate).astype(BF)
        pack(dot(w_out[...], d_proj, 1, 0) * gain, first, scr)
        for which, weights in enumerate((w_left, w_right)):
            value = dot(weights[...], zn, 0, 0)
            sigma = sigmoid(value[128:])
            factors[which * 256 : which * 256 + 128, here] = (mask * sigma).astype(BF)
            factors[which * 256 + 128 : which * 256 + 256, here] = (mask * value[:128] * sigma * (1.0 - sigma)).astype(BF)
    hat_grad[...] = packed(scr, F32)


def gather_map(got, which, scr):
    for r in range(8):
        for c in range(8):
            scr[r * 64 : (r + 1) * 64, c * 128 : (c + 1) * 128] = got[r * 8 + c, which]


def double_rows(got, which, scr):
    low = low_half((64, 128))
    zero = jnp.zeros((64, 128), BF)
    for r in range(8):
        for c in range(8):
            tile = got[r * 8 + c, which]
            lanes = slice(c * 128, (c + 1) * 128)
            scr[r * 128 : r * 128 + 64, lanes] = jnp.where(low, tile, zero)
            scr[r * 128 + 64 : (r + 1) * 128, lanes] = jnp.where(low, zero, tile)


def product_kernel(got, send, a_scr, b_scr, out_scr, sems):
    gather_map(got, 0, a_scr)
    double_rows(got, 1, b_scr)
    copies = []
    for n in range(4):
        out = dot(a_scr[...], b_scr[n * 256 : (n + 1) * 256, :], 1, 1).astype(BF)
        for r in range(8):
            for c in range(2):
                out_scr[r, 2 * n + c] = out[r * 64 : (r + 1) * 64, c * 128 : (c + 1) * 128]
        part = (slice(None), pl.ds(2 * n, 2))
        copies.append(pltpu.make_async_copy(out_scr.at[part], send.at[part], sems.at[n]))
        copies[-1].start()
    for copy in copies:
        copy.wait()


def halves_sum(values):
    return values + pltpu.roll(values, 64, 1)


def middle_kernel(got, hat_grad, send):
    rows = pl.ds(pl.multiple_of(pl.program_id(0) * STEP, STEP), STEP)

    def value(d):
        return got[d, rows].astype(F32)

    def channel_mean(term):
        sums = [term(d) for d in range(4)]
        for d in range(4, 64):
            sums[d % 4] = sums[d % 4] + term(d)
        return halves_sum((sums[0] + sums[1]) + (sums[2] + sums[3])) * (1.0 / 128)

    mean = channel_mean(value)
    inverse = lax.rsqrt(channel_mean(lambda d: (value(d) - mean) * (value(d) - mean)) + EPS)
    first = channel_mean(lambda d: hat_grad[d])
    second = channel_mean(lambda d: hat_grad[d] * ((value(d) - mean) * inverse))
    for d in range(64):
        hat = (value(d) - mean) * inverse
        send[d, rows] = (inverse * (hat_grad[d] - first - hat * second)).astype(BF)


def updated_kernel(
    product, zn_ref, cot, gain_ref, bias_ref, w_out, w_gate,
    updated, dg_out, grad_out, grad_gate, scr,
):
    @pl.when(pl.program_id(0) == 0)
    def _():
        grad_out[...] = jnp.zeros((128, 128), F32)
        grad_gate[...] = jnp.zeros((128, 128), F32)

    spread(product[...], scr)
    gain, bias = column(gain_ref), column(bias_ref)
    for first, here in spans(ROWS):
        hat, _ = normalize(unpack(scr, first, ROWS))
        y = (hat * gain + bias).astype(BF)
        zn = zn_ref[:, here]
        gate = sigmoid(dot(w_gate[...], zn, 0, 0))
        upstream = load_transposed(cot, first, ROWS)
        proj = dot(w_out[...], y, 0, 0)
        d_proj = (upstream * gate).astype(BF)
        d_gpre = (upstream * proj * gate * (1.0 - gate)).astype(BF)
        store_transposed(updated, first, gate * proj)
        dg_out[:, here] = d_gpre
        grad_out[...] += dot(y, d_proj, 1, 1)
        grad_gate[...] += dot(zn, d_gpre, 1, 1)


def product_grads_kernel(got, operands_ref, send, a_scr, b_scr, d_scr, out_scr, sems):
    def copy(which, first, count, sem):
        part = (pl.ds(first, count), which)
        return pltpu.make_async_copy(out_scr.at[part], send.at[part], sems.at[sem])

    copies = [copy(0, 0, 64, 0), copy(1, 0, 32, 1), copy(1, 32, 32, 2)]

    gather_map(operands_ref, 0, a_scr)
    double_rows(operands_ref, 1, b_scr)
    for r in range(8):
        for c in range(8):
            d_scr[r * 64 : (r + 1) * 64, c * 128 : (c + 1) * 128] = got[r * 8 + c]
    for n in range(4):
        out = dot(d_scr[...], b_scr[:, n * 256 : (n + 1) * 256], 1, 0).astype(BF)
        for r in range(8):
            for c in range(2):
                out_scr[r * 8 + 2 * n + c, 0] = out[r * 64 : (r + 1) * 64, c * 128 : (c + 1) * 128]
    copies[0].start()
    low = low_half((64, 128))
    for m in range(2):
        out = dot(d_scr[:, m * 512 : (m + 1) * 512], a_scr[...], 0, 0)
        for r in range(4):
            for c in range(8):
                lanes = slice(c * 128, (c + 1) * 128)
                out_scr[(m * 4 + r) * 8 + c, 1] = jnp.where(
                    low, out[r * 128 : r * 128 + 64, lanes], out[r * 128 + 64 : (r + 1) * 128, lanes]
                ).astype(BF)
        copies[1 + m].start()
    for started in copies:
        started.wait()


def cell_grads(got, which, factors, scr):
    rows = pl.ds(pl.multiple_of(pl.program_id(0) * STEP, STEP), STEP)
    spread(got[:, which, rows], scr)
    grad = unpack(scr, 0, STEP)
    slope = factors[which * 256 : which * 256 + 128]
    bend = factors[which * 256 + 128 : which * 256 + 256]
    return jnp.concatenate([grad * slope, grad * bend], axis=0).astype(BF)


def weights_kernel(
    got, zn_cells, factors, grad_gate, grad_out, send, acc, stage, scr
):
    @pl.when(pl.program_id(0) == 0)
    def _():
        acc[...] = jnp.zeros((512, 128), F32)

    for which in range(2):
        grads = cell_grads(got, which, factors, scr)
        acc[which * 256 : (which + 1) * 256] += dot(grads, zn_cells[...], 1, 0)

    @pl.when(pl.program_id(0) == pl.num_programs(0) - 1)
    def _():
        for t in range(6):
            if t < 4:
                tile = acc[t * 128 : (t + 1) * 128]
            else:
                tile = (grad_gate if t == 4 else grad_out)[...]
            for half in range(2):
                stage[pl.ds(2 * t + half, 64, stride=PITCH_16), :] = tile[half * 64 : (half + 1) * 64]
        for t in range(12, 16):
            stage[pl.ds(t, 64, stride=PITCH_16), :] = jnp.zeros((64, 128), F32)
        send[...] = jnp.stack([stage[d * PITCH_16 : d * PITCH_16 + 16] for d in range(64)]).astype(BF)


def pair_kernel(pair, gain_ref, got, factors, dg, w_left, w_right, w_gate, out, scr):
    gain = column(gain_ref)
    d_left = cell_grads(got, 0, factors, scr)
    d_right = cell_grads(got, 1, factors, scr)
    for first, here in spans(ROWS):
        zhat, inverse = normalize(load_transposed(pair, first, ROWS))
        d_zn = (
            dot(w_left[...], d_left[:, here], 1, 0)
            + dot(w_right[...], d_right[:, here], 1, 0)
            + dot(w_gate[...], dg[:, here], 1, 0)
        )
        store_transposed(out, first, normalize_backward(d_zn * gain, zhat, inverse))


def sum_kernel(scale, got, send):
    total = got[0].astype(F32)
    for s in range(1, 64):
        total = total + got[s].astype(F32)
    send[...] = jnp.broadcast_to((total * scale).astype(BF)[None], send.shape)


def split_kernel(got, left, right, gate, out, stage):
    wide = got[...].astype(F32)
    for d in range(64):
        stage[d * PITCH_16 : d * PITCH_16 + 16] = wide[d]
    for t, (ref, lane) in enumerate(
        ((left, 0), (left, 128), (right, 0), (right, 128), (gate, 0), (out, 0))
    ):
        tile = jnp.concatenate(
            [stage[pl.ds(2 * t + half, 64, stride=PITCH_16), :] for half in range(2)], axis=0
        )
        ref[:, lane : lane + 128] = jnp.transpose(tile) if t < 4 else tile


def call(kernel, grid, in_specs, out_specs, out_shape, scratch=(), cost=(10**9, 10**7)):
    return pl.pallas_call(
        kernel,
        grid=grid,
        in_specs=in_specs,
        out_specs=out_specs,
        out_shape=out_shape,
        scratch_shapes=list(scratch),
        cost_estimate=pl.CostEstimate(flops=cost[0], bytes_accessed=cost[1], transcendentals=0),
        compiler_params=pltpu.CompilerParams(vmem_limit_bytes=LIMIT),
    )


def whole(*dims):
    return pl.BlockSpec(dims, lambda *_: (0,) * len(dims))


def shape(dims, kind, space=None):
    return jax.ShapeDtypeStruct(dims, kind) if space is None else space(dims, kind)


def keep(value, space):
    return pltpu.with_memory_space_constraint(value, space)


def exchange(values):
    owners = values.shape[0]
    flat = values.reshape(owners, -1, 128)
    return lax.all_to_all(flat, AXES, 0, 0, tiled=True).reshape(values.shape)


def body(
    pair, length, ln_in_gain, ln_in_bias, w_left, w_right, w_gate,
    product_norm_gain, product_norm_bias, w_out, cotangent,
):
    tile_i, tile_j, chans = pair.shape
    total = tile_j * lax.axis_size("col")
    cells = tile_i * tile_j
    grid = (tile_i // STEP,)
    gain_in, bias_in = ln_in_gain.reshape(1, 128), ln_in_bias.reshape(1, 128)
    gain_p, bias_p = product_norm_gain.reshape(1, 128), product_norm_bias.reshape(1, 128)
    pair, cotangent = keep(pair, pltpu.HBM), keep(cotangent, pltpu.HBM)
    w_left, w_right, w_gate, w_out = (
        keep(w, pltpu.HBM) for w in (w_left, w_right, w_gate, w_out)
    )

    natural = pl.BlockSpec((STEP, 64, 128), lambda i: (i, 0, 0))
    chan_major = pl.BlockSpec((128, CELLS), lambda i: (0, i))
    chan_major4 = pl.BlockSpec((512, CELLS), lambda i: (0, i))
    cell_major = pl.BlockSpec((CELLS, 128), lambda i: (i, 0))
    single = pl.BlockSpec((64, STEP, 128), lambda i: (0, i, 0))
    double = pl.BlockSpec((64, 2, STEP, 128), lambda i: (0, 0, i, 0))
    direct = pl.BlockSpec(memory_space=pltpu.VMEM)
    scalar = pl.BlockSpec(memory_space=pltpu.SMEM)
    vec, wide, square = whole(1, 128), whole(128, 256), whole(128, 128)
    swap = pltpu.VMEM((66 * PITCH - 2, 128), F32)
    near, far = pltpu.VMEM, pltpu.HBM
    b_cells = shape((128, cells), BF, far)
    f_square = shape((128, 128), F32, far)
    a_map, b_map = pltpu.VMEM((512, 1024), BF), pltpu.VMEM((1024, 1024), BF)

    send, zn = call(
        operands_kernel, grid,
        [natural, scalar, vec, vec, wide, wide],
        [direct, chan_major],
        [shape((64, 2, 64, 128), BF, near), b_cells],
        [swap] * 2,
    )(pair, length, gain_in, bias_in, w_left, w_right)
    zn = keep(zn, far)
    operands = keep(exchange(send), near)

    factors, hat_grad, zn_cells = call(
        factors_kernel, grid,
        [chan_major, scalar, natural, vec, wide, wide, square, square],
        [chan_major4, single, cell_major],
        [shape((512, cells), BF, far), shape((64, 64, 128), F32, far), shape((cells, 128), BF, far)],
        [swap],
    )(zn, length, cotangent, gain_p, w_left, w_right, w_gate, w_out)
    factors = keep(factors, far)

    product = call(
        product_kernel, (1,),
        [direct],
        pl.BlockSpec(memory_space=pltpu.HBM),
        shape((8, 8, 64, 128), BF, far),
        [a_map, b_map, pltpu.VMEM((8, 8, 64, 128), BF), pltpu.SemaphoreType.DMA((4,))],
    )(operands).reshape(64, 64, 128)

    product = keep(exchange(product), near)
    send = call(
        middle_kernel, grid,
        [direct, single],
        direct,
        shape((64, 64, 128), BF, near),
    )(product, keep(hat_grad, far))
    got = exchange(send)

    updated, d_gpre, grad_out, grad_gate = call(
        updated_kernel, grid,
        [single, chan_major, natural, vec, vec, square, square],
        [natural, chan_major, square, square],
        [shape(pair.shape, BF, far), b_cells, f_square, f_square],
        [swap],
    )(product, zn, cotangent, gain_p, bias_p, w_out, w_gate)

    send = call(
        product_grads_kernel, (1,),
        [direct, direct],
        pl.BlockSpec(memory_space=pltpu.HBM),
        shape((64, 2, 64, 128), BF, far),
        [a_map, b_map, a_map, pltpu.VMEM((64, 2, 64, 128), BF), pltpu.SemaphoreType.DMA((3,))],
    )(keep(got, near), operands)

    grads = keep(exchange(send), near)
    terms = call(
        weights_kernel, grid,
        [direct, cell_major, chan_major4] + [square, square],
        whole(64, 16, 128),
        shape((64, 16, 128), BF, far),
        [pltpu.VMEM((512, 128), F32), pltpu.VMEM((66 * PITCH_16 - 2, 128), F32), swap],
    )(grads, keep(zn_cells, far), factors, keep(grad_gate, far), keep(grad_out, far))
    shares = exchange(terms)

    d_pair = call(
        pair_kernel, grid,
        [natural, vec, direct, chan_major4, chan_major] + [wide, wide, square],
        natural,
        shape(pair.shape, BF, far),
        [swap],
    )(pair, gain_in, grads, factors, keep(d_gpre, far), w_left, w_right, w_gate)

    summed = call(
        functools.partial(sum_kernel, 1.0 / total), (1,),
        [direct], whole(64, 16, 128), shape((64, 16, 128), BF, far), cost=(10**6, 10**6),
    )(keep(shares, near))
    sums = call(
        split_kernel, (1,),
        [whole(64, 16, 128)],
        [wide, wide, square, square],
        [shape((128, 256), F32)] * 2 + [shape((128, 128), F32)] * 2,
        [pltpu.VMEM((66 * PITCH_16 - 2, 128), F32)],
        cost=(10**6, 10**6),
    )(exchange(summed))
    return (updated, d_pair, *sums)


def solution(mesh):
    in_specs = (
        P(("rep", "row"), "col", None),
        P("rep"),
        P(),
        P(),
        P(),
        P(),
        P(),
        P(),
        P(),
        P(),
        P(("rep", "row"), "col", None),
    )
    out_specs = (
        P(("rep", "row"), "col", None),
        P(("rep", "row"), "col", None),
        P("rep", None),
        P("rep", None),
        P("rep", None),
        P("rep", None),
    )
    return jax.shard_map(body, mesh=mesh, in_specs=in_specs, out_specs=out_specs, check_vma=False)
```
